32 devices in a mesh: dp: 32 (over z, y, x, core).
Axes of the slice: x: 2, y: 2, z: 4, core: 2. Of those that a mesh axis runs over, the one named last changes fastest.
Arguments:
- bin_index: int32 [65536, 256], P('dp'), may hold values from 0 to 63
- node_ids: int32 [65536], P('dp'), may hold values from 0 to 1
- gradients: bfloat16 [65536, 32], P('dp'), may hold values from -6 to 6
- hessians: bfloat16 [65536, 32], P('dp'), may hold values from 0.02 to 0.25
Outputs:
- gains: float32 [256, 2, 64], replicated
- weights: float32 [256, 2, 64, 32], replicated
The draws below stay inside these ranges and needn't reach their ends.
All inputs are finite; a program needn't handle non-finite values.
Results may differ from the reference program's by a relative error of at most 0.0003.
Values sent between devices are 32-bit elements; how exact they have to be, the bound alone decides.
No kernel may reach another device: no remote copies, remote signals or barrier semaphores. Data moves between devices by JAX's collectives and lax.ppermute only.
A program may use at most 128 MiB of HBM per device.

```python
import math
import jax
import jax.numpy as jnp
from jax import lax

F = 256
B = 64
K = 32
NODES = 2
ROWS = 65536


def latent_level(key):
    row_order = jax.random.permutation(jax.random.fold_in(key, 11), ROWS).astype(jnp.int32)
    row_level = (row_order % B).astype(jnp.int32)
    return (row_order, row_level)


def draw_bin_index(key, part):
    row_order, row_level = latent_level(key)
    subkeys = jax.random.split(jax.random.fold_in(key, 23), 3)
    strides = 2 * jax.random.randint(subkeys[0], (F,), 0, B // 2) + 1
    offsets = jax.random.randint(subkeys[1], (F,), 0, B)
    jitters = jax.random.randint(subkeys[2], (ROWS, F), 0, max(B // 4, 2))
    jitters = jitters * (row_order >= B).astype(jnp.int32)[:, None]
    mixed = row_level[:, None] * strides[None, :] + offsets[None, :] + jitters
    return (mixed % B).astype(jnp.int32)


def draw_hessians(key, part):
    row_order, row_level = latent_level(key)
    subkeys = jax.random.split(jax.random.fold_in(key, 31), 2)
    level_table = jnp.exp(jax.random.uniform(subkeys[0], (B, K), jnp.float32, math.log(0.03), math.log(0.2)))
    row_factor = jax.random.uniform(subkeys[1], (ROWS, K), jnp.float32, 0.75, 1.2)
    values = level_table[row_level] * row_factor
    return values.astype(jnp.bfloat16)


def plant(array, rng, low, high):
    longest = array.shape.index(max(array.shape))
    spots = []
    for shift in (0, 1):
        where = [jax.random.randint(jax.random.fold_in(rng, axis), (), 0, length) for axis, length in enumerate(array.shape)]
        where[longest] = (where[longest] + shift) % array.shape[longest]
        spots.append(tuple(where))
    return array.at[spots[0]].set(low).at[spots[1]].set(high)


def shard_levels(own_key, dims, pieces, low, largest):
    gain, own = 1.0, jax.random.fold_in(own_key, 6)
    for position, blocks in pieces:
        steps = jnp.exp(jax.random.uniform(jax.random.fold_in(own, position), (blocks,), jnp.float32, low / len(pieces), largest / len(pieces)))
        gain = gain * jnp.repeat(steps, dims[position] // blocks).reshape([-1 if axis == position else 1 for axis in range(len(dims))])
    return gain


def gaussian(stream_key, dims, scale, most, shards=(), held_as=jnp.bfloat16):
    values = jax.random.normal(stream_key, dims, jnp.float32) * scale
    if len(shards) > 0:
        values = shard_levels(stream_key, dims, shards, -0.22, 0.18) * values
    return jnp.clip(values, min=-most, max=most).astype(held_as)


def setup_inputs(seed: int = 0) -> dict:
    seeds = jax.random.split(jax.random.key(seed), 5)
    return {
        "bin_index": draw_bin_index(jax.random.fold_in(seeds[4], 71), 0),
        "node_ids": plant(jax.random.randint(seeds[1], (ROWS,), 0, NODES), jax.random.fold_in(seeds[1], 1), 0, NODES - 1).astype(jnp.int32),
        "gradients": gaussian(seeds[2], (ROWS, K), 1.0, 6.0, ((0, 32),)),
        "hessians": draw_hessians(jax.random.fold_in(seeds[4], 71), 0),
    }


RIDGE = 1.0


def curves(hist):
    width = hist.shape[-1] // 2
    running = jnp.cumsum(hist, axis=2)
    totals = running[:, :, -1:, :]
    right_side = totals - running

    def score(part):
        return part[..., :width] * part[..., :width] / (part[..., width:] + RIDGE)

    gains = jnp.mean(score(running) + score(right_side) - score(totals), axis=-1)
    weights = -running[..., :width] / (running[..., width:] + RIDGE)
    return gains, weights


def reference(bin_index, node_ids, gradients, hessians):
    paired = jnp.concatenate([gradients, hessians], axis=1).astype(jnp.float32)

    def one_feature(column):
        segment = (node_ids * B + column).astype(jnp.int32)
        summed = jax.ops.segment_sum(paired, segment, num_segments=NODES * B)
        return summed.reshape(NODES, B, 2 * K)

    hist = lax.map(one_feature, bin_index.T)
    gains, weights = curves(hist)
    return gains, weights
```

```python
import functools

import jax
import jax.numpy as jnp
from jax import lax
from jax.experimental import pallas as pl
from jax.experimental.pallas import tpu as pltpu
from jax.sharding import PartitionSpec as P

B = 64
K = 32
NODES = 2
RIDGE = 1.0
LANES = 128
EXTRA = 8
VMEM_LIMIT = 48 * 2**20


class Plan:
    def __init__(self, devices):
        bits = devices.bit_length() - 1
        assert devices == 1 << bits and bits >= 4
        self.items = devices // 2
        self.bin_bits = bits - 2
        self.unit = 1 << self.bin_bits
        self.units = B // self.unit
        assert self.units >= 1
        first = [((2,), (4,)), ((4,), (2,))]
        rest = list(range(3, bits))
        later = []
        while rest:
            now, rest = rest[:2], rest[2:]
            masks = tuple(1 << b for b in now)
            later.append((masks, masks))
        self.stages = first + later
        self.flips = [[], []]
        for core in (0, 1):
            for stage in reversed(self.stages):
                self.flips[core].extend(stage[core])
        self.half_at = self.flips[0].index(devices // 2)
        assert self.flips[1][self.half_at] == devices // 2

    def mirrored(self, item):
        top = len(self.flips[0]) - 1
        differ = ((item >> top) ^ (item >> (top - 1))) & 1
        return item ^ (differ * (3 << (top - 1)))

    def sizes(self):
        share = self.units // 4
        return [share] * 4 if share else [1] * self.units

    def groups(self, stage):
        return 1 << len(self.stages[stage][0])

    def partner(self, stage, group, device):
        flip = 0
        for i, mask in enumerate(self.stages[stage][device & 1]):
            flip ^= mask * ((group >> i) & 1)
        return device ^ flip

    def mask(self, item, core):
        total = 0
        for i, (even, odd) in enumerate(zip(*self.flips, strict=True)):
            total = total ^ (((item >> i) & 1) * (even + core * (odd - even)))
        return total


def hist_body(plan, first_unit, count, has_totals, bins, spread, keep, send):
    me = lax.axis_index("dp")
    core = me & 1
    rows = bins.shape[0]
    step = min(rows, 256)
    half_at = plan.half_at
    low = (1 << half_at) - 1

    @pl.loop(0, plan.items // 2)
    def _(slot):
        item = ((slot >> half_at) << (half_at + 1)) | (slot & low)
        other = item | (1 << half_at)
        owner = (me ^ plan.mask(item, core)) >> 1
        low_bin = owner & (plan.unit - 1)
        for u in range(count):
            level = (first_unit + u) * plan.unit + low_bin
            level = level.astype(jnp.float32).astype(jnp.bfloat16)
            total = jnp.zeros((spread.shape[0], bins.shape[1]), jnp.float32)
            for start in range(0, rows, step):
                below = jnp.where(
                    bins[start : start + step, :] <= level, jnp.bfloat16(1), jnp.bfloat16(0)
                )
                total += jnp.dot(
                    spread[:, start : start + step], below, preferred_element_type=jnp.float32
                )
            at = pl.ds(u * 2 * K, 2 * K)
            keep[item, at, :] = total[: 2 * K, :LANES]
            keep[other, at, :] = total[: 2 * K, LANES:]
            send[plan.mirrored(item), at, :] = total[2 * K :, :LANES]
            send[plan.mirrored(other), at, :] = total[2 * K :, LANES:]
    if has_totals:
        sums = jnp.sum(spread[...].astype(jnp.float32), axis=1, keepdims=True)
        lane = lax.broadcasted_iota(jnp.int32, (EXTRA, LANES), 1)
        for target, base in ((keep, 0), (send, 2 * K)):
            packed = jnp.zeros((EXTRA, LANES), jnp.float32)
            for i in range(2 * K // EXTRA):
                part = sums[base + i * EXTRA : base + (i + 1) * EXTRA, :]
                packed = jnp.where(lane == i, part, packed)
            for item in range(plan.items):
                target[item, pl.ds(count * 2 * K, EXTRA), :] = packed


def first_kernel(plan, count, bins_ref, node_ref, grad_ref, hess_ref, keep, send, bins, spread):
    me = lax.axis_index("dp")
    core = me & 1
    half = me >> (plan.bin_bits + 1)
    raw = bins_ref[...].astype(jnp.float32).astype(jnp.bfloat16)
    swapped = jnp.concatenate([raw[:, LANES:], raw[:, :LANES]], axis=1)
    bins[...] = jnp.where(half == 0, raw, swapped)
    paired = jnp.concatenate([grad_ref[...], hess_ref[...]], axis=0).astype(jnp.float32)
    node = node_ref[...]
    for slot in range(NODES):
        here = (node == (core ^ slot)).astype(jnp.float32)
        spread[slot * 2 * K : (slot + 1) * 2 * K, :] = (paired * here).astype(jnp.bfloat16)
    hist_body(plan, 0, count, True, bins, spread, keep, send)


def next_kernel(plan, first_unit, count, bins, spread, keep, send):
    hist_body(plan, first_unit, count, False, bins, spread, keep, send)


def vmem(n):
    return [pl.BlockSpec(memory_space=pltpu.VMEM)] * n


def call(body, out_shape, n_in, flops=0, moved=0):
    return pl.pallas_call(
        body,
        out_shape=out_shape,
        in_specs=vmem(n_in),
        out_specs=vmem(len(out_shape)),
        compiler_params=pltpu.CompilerParams(vmem_limit_bytes=VMEM_LIMIT),
        cost_estimate=pl.CostEstimate(flops=flops, bytes_accessed=moved, transcendentals=0),
    )


def f32(*shape):
    return jax.ShapeDtypeStruct(shape, jnp.float32)


def add_body(mine, theirs, *outs):
    each = outs[0].shape[0]
    for i, out in enumerate(outs):
        out[...] = mine[i * each : (i + 1) * each] + theirs[i * each : (i + 1) * each]


def add_split(mine, theirs, groups):
    items, rows, lanes = mine.shape
    return call(
        add_body, [f32(items // groups, rows, lanes)] * groups, 2, moved=mine.size * 12
    )(mine, theirs)


def score(g, h):
    return g * g / (h + RIDGE)


def curves_body(count, first_unit, has_totals, last, n_parts, *refs):
    parts, refs = refs[:n_parts], refs[n_parts:]
    if has_totals:
        weights, totals, gains = refs
    elif last:
        packed, old_gains, weights = refs
    else:
        packed, old_gains, weights, gains = refs

    def summed(start, size):
        total = parts[0][0, start : start + size, :]
        for part in parts[1:]:
            total += part[0, start : start + size, :]
        return total

    if has_totals:
        block = summed(count * 2 * K, EXTRA)
        totals[...] = block
        gain_rows = jnp.zeros((EXTRA, LANES), jnp.float32)
    else:
        block = packed[...]
        gain_rows = old_gains[...]
    columns = [
        jnp.broadcast_to(block[:, i : i + 1], (EXTRA, LANES)) for i in range(2 * K // EXTRA)
    ]
    row = lax.broadcasted_iota(jnp.int32, (EXTRA, LANES), 0)
    for u in range(count):
        gain = jnp.zeros((EXTRA, LANES), jnp.float32)
        for i in range(K // EXTRA):
            gl = summed(u * 2 * K + i * EXTRA, EXTRA)
            hl = summed(u * 2 * K + K + i * EXTRA, EXTRA)
            g, h = columns[i], columns[K // EXTRA + i]
            gain += score(gl, hl) + score(g - gl, h - hl) - score(g, h)
            weights[0, u * K + i * EXTRA : u * K + (i + 1) * EXTRA, :] = -gl / (hl + RIDGE)
        mean = jnp.sum(gain, axis=0, keepdims=True) / K
        gain_rows = jnp.where(row == first_unit + u, mean, gain_rows)
    if last:
        weights[0, count * K : count * K + EXTRA, :] = gain_rows
    else:
        gains[...] = gain_rows


def place_body(plan, first_unit, count, last, first, *refs):
    if not first:
        refs = refs[1:]
    mine, theirs, weights = refs[:3]
    if last:
        gains, held, lines, sems, held_sems = refs[3:]
    else:
        (sems,) = refs[3:]
    me = lax.axis_index("dp")
    copies = []
    fetched = []
    for side, source in enumerate((mine, theirs)):
        who = me ^ side
        core = who & 1
        if last:
            fetch = pltpu.make_async_copy(
                source.at[:, pl.ds(count * K, EXTRA), :], held.at[side], held_sems.at[side]
            )
            fetch.start()
            fetched.append(fetch)
        for item in range(plan.items):
            owner = (who ^ plan.mask(item, core)) >> 1
            low_bin = owner & (plan.unit - 1)
            half = owner >> plan.bin_bits
            at = pl.multiple_of(half * LANES, LANES)
            for u in range(count):
                copy = pltpu.make_async_copy(
                    source.at[item, pl.ds(u * K, K), :],
                    weights.at[core, (first_unit + u) * plan.unit + low_bin, :, pl.ds(at, LANES)],
                    sems.at[(side * plan.items + item) * count + u],
                )
                copy.start()
                copies.append(copy)
    if last:
        for side in range(2):
            fetched[side].wait()
        for side in range(2):
            who = me ^ side
            core = who & 1
            for item in range(plan.items):
                owner = (who ^ plan.mask(item, core)) >> 1
                low_bin = owner & (plan.unit - 1)
                half = owner >> plan.bin_bits
                for u in range(plan.units):
                    value = held[side, item, u : u + 1, :]
                    lines[core, half, pl.ds(u * plan.unit + low_bin, 1), :] = value
        for h in range(2):
            gains[:, :, h * LANES : (h + 1) * LANES] = lines[:, h]
    for copy in copies:
        copy.wait()


def place(plan, first_unit, count, last, buffer, mine, theirs, features):
    first = buffer is None
    out_shape = [f32(NODES, B, K, features)]
    out_specs = [pl.BlockSpec(memory_space=pl.ANY)]
    scratch = [pltpu.SemaphoreType.DMA((2 * plan.items * count,))]
    if last:
        out_shape.append(f32(NODES, B, features))
        out_specs.append(pl.BlockSpec(memory_space=pltpu.VMEM))
        scratch = [
            pltpu.VMEM((2, plan.items, EXTRA, LANES), jnp.float32),
            pltpu.VMEM((NODES, 2, B, LANES), jnp.float32),
            *scratch,
            pltpu.SemaphoreType.DMA((2,)),
        ]
    operands = [mine, theirs] if first else [buffer, mine, theirs]
    return pl.pallas_call(
        functools.partial(place_body, plan, first_unit, count, last, first),
        out_shape=out_shape,
        in_specs=[pl.BlockSpec(memory_space=pl.ANY)] * len(operands),
        out_specs=out_specs,
        scratch_shapes=scratch,
        input_output_aliases={} if first else {0: 0},
        compiler_params=pltpu.CompilerParams(vmem_limit_bytes=VMEM_LIMIT),
        cost_estimate=pl.CostEstimate(flops=0, bytes_accessed=mine.size * 16, transcendentals=0),
    )(*operands)


def on_device(bin_index, node_ids, gradients, hessians):
    devices = lax.axis_size("dp")
    plan = Plan(devices)
    rows, features = bin_index.shape
    assert features == 2 * LANES

    def swap(x, stage, group):
        pairs = [(d, plan.partner(stage, group, d)) for d in range(devices)]
        return lax.ppermute(x, "dp", pairs)

    def swap_cores(x):
        return lax.ppermute(x, "dp", [(d, d ^ 1) for d in range(devices)])

    sizes = plan.sizes()
    starts = [sum(sizes[:i]) for i in range(len(sizes))]
    totals = gains = buffer = gains_out = None
    bins = spread = None
    for number, (first_unit, count) in enumerate(zip(starts, sizes, strict=True)):
        last = number == len(sizes) - 1
        depth = count * 2 * K + (EXTRA if number == 0 else 0)
        halves = [f32(plan.items, depth, LANES)] * 2
        work = 2 * rows * features * 4 * K * plan.items // 2 * count
        if number == 0:
            keep, send, bins, spread = call(
                functools.partial(first_kernel, plan, count),
                [
                    *halves,
                    jax.ShapeDtypeStruct((rows, features), jnp.bfloat16),
                    jax.ShapeDtypeStruct((NODES * 2 * K, rows), jnp.bfloat16),
                ],
                4,
                flops=3 * work,
            )(bin_index, node_ids.reshape(1, rows), gradients.T, hessians.T)
        else:
            keep, send = call(
                functools.partial(next_kernel, plan, first_unit, count), halves, 2, flops=3 * work
            )(bins, spread)
        held = add_split(keep, swap_cores(send), plan.groups(0))
        for stage in range(len(plan.stages)):
            got = [swap(held[g], stage, g) for g in range(1, plan.groups(stage))]
            if stage == len(plan.stages) - 1:
                break
            mine = held[0]
            for extra in got[:-1]:
                mine = mine + extra
            held = add_split(mine, got[-1], plan.groups(stage + 1))
        parts = [held[0], *got]
        body = functools.partial(
            curves_body, count, first_unit, number == 0, last and number > 0, len(parts)
        )
        tile = f32(EXTRA, LANES)
        if number == 0:
            weights, totals, gains = call(body, [f32(1, count * K, LANES), tile, tile], len(parts))(
                *parts
            )
            if last:
                weights = jnp.concatenate([weights, gains[None]], axis=1)
        elif last:
            (weights,) = call(body, [f32(1, count * K + EXTRA, LANES)], len(parts) + 2)(
                *parts, totals, gains
            )
        else:
            weights, gains = call(body, [f32(1, count * K, LANES), tile], len(parts) + 2)(
                *parts, totals, gains
            )
        for stage in reversed(range(len(plan.stages))):
            weights = jnp.concatenate(
                [weights, *(swap(weights, stage, g) for g in range(1, plan.groups(stage)))], axis=0
            )
        placed = place(
            plan, first_unit, count, last, buffer, weights, swap_cores(weights), features
        )
        buffer = placed[0]
        if last:
            gains_out = placed[1]
    return gains_out.transpose(2, 0, 1), buffer.transpose(3, 0, 1, 2)


def solution(mesh):
    return jax.shard_map(
        on_device,
        mesh=mesh,
        in_specs=(P("dp", None), P("dp"), P("dp", None), P("dp", None)),
        out_specs=(P(), P()),
        check_vma=False,
    )
```

```python
import functools

import jax
import jax.numpy as jnp
from jax import lax
from jax.experimental import pallas as pl
from jax.experimental.pallas import tpu as pltpu
from jax.sharding import PartitionSpec as P

B = 64
K = 32
NODES = 2
RIDGE = 1.0
LANES = 128
EXTRA = 8
VMEM_LIMIT = 48 * 2**20
SIZES = [2, 2, 2, 2]
BUNDLES = [[0], [1], [2], [3]]
BATCHES = [[0, 1], [2], [3]]


class Plan:
    def __init__(self, devices):
        bits = devices.bit_length() - 1
        assert devices == 1 << bits and bits >= 4
        self.top = devices // 2
        self.unit = self.items = devices // 4
        self.units = B // self.unit
        assert self.units >= 1
        self.stages = [(2, 4), (4, 2)] + [(1 << b, 1 << b) for b in range(3, bits - 1)]

    def partner(self, stage, device):
        return device ^ self.stages[stage][device & 1]

    def mask(self, item, core):
        total = 0
        for i, (even, odd) in enumerate(reversed(self.stages)):
            total = total ^ (((item >> i) & 1) * (even + core * (odd - even)))
        return total

    def low_bin(self, device, item):
        return ((device ^ self.mask(item, device & 1)) >> 1) & (self.unit - 1)

    def mirrored(self, item):
        at = len(self.stages) - 2
        differ = ((item >> at) ^ (item >> (at + 1))) & 1
        return item ^ (differ * (3 << at))

    def sizes(self):
        if self.units == 8:
            return SIZES, BUNDLES, BATCHES
        return [self.units], [[0]], [[0]]


def hist_body(plan, first_unit, count, has_totals, bins, spread, keep, send):
    me = lax.axis_index("dp")
    rows = bins.shape[0]
    step = min(rows, 256)

    @pl.loop(0, plan.items)
    def _(item):
        low_bin = plan.low_bin(me, item)
        for u in range(count):
            level = (first_unit + u) * plan.unit + low_bin
            level = level.astype(jnp.float32).astype(jnp.bfloat16)
            total = jnp.zeros((spread.shape[0], bins.shape[1]), jnp.float32)
            for start in range(0, rows, step):
                below = jnp.where(
                    bins[start : start + step, :] <= level, jnp.bfloat16(1), jnp.bfloat16(0)
                )
                total += jnp.dot(
                    spread[:, start : start + step], below, preferred_element_type=jnp.float32
                )
            at = pl.ds(u * 2 * K, 2 * K)
            keep[item, at, :] = total[: 2 * K, :]
            send[plan.mirrored(item), at, :] = total[2 * K :, :]

    if has_totals:
        sums = jnp.sum(spread[...].astype(jnp.float32), axis=1, keepdims=True)
        lane = lax.broadcasted_iota(jnp.int32, (EXTRA, bins.shape[1]), 1)
        for target, base in ((keep, 0), (send, 2 * K)):
            packed = jnp.zeros((EXTRA, bins.shape[1]), jnp.float32)
            for i in range(2 * K // EXTRA):
                part = sums[base + i * EXTRA : base + (i + 1) * EXTRA, :]
                packed = jnp.where(lane == i, part, packed)
            for item in range(plan.items):
                target[item, pl.ds(count * 2 * K, EXTRA), :] = packed


def first_kernel(plan, count, blocks, *refs):
    bins_in, node_in, grad_in, hess_in, keep, send, bins, spread = refs[:8]
    raw, node, paired, sems = refs[8:]
    me = lax.axis_index("dp")
    core = me & 1
    step = bins.shape[0] // blocks
    width = grad_in.shape[0]
    small = [
        pltpu.make_async_copy(node_in, node, sems.at[0]),
        pltpu.make_async_copy(grad_in, paired.at[pl.ds(0, width), :], sems.at[1]),
        pltpu.make_async_copy(hess_in, paired.at[pl.ds(width, width), :], sems.at[2]),
    ]
    large = [
        pltpu.make_async_copy(
            bins_in.at[pl.ds(i * step, step), :], raw.at[pl.ds(i * step, step), :], sems.at[3 + i]
        )
        for i in range(blocks)
    ]
    for copy in small + large:
        copy.start()
    for copy in small:
        copy.wait()
    for slot in range(NODES):
        here = (node[...] == (core ^ slot)).astype(jnp.float32)
        spread[slot * 2 * K : (slot + 1) * 2 * K, :] = (
            paired[...].astype(jnp.float32) * here
        ).astype(jnp.bfloat16)
    for i, copy in enumerate(large):
        copy.wait()
        at = slice(i * step, (i + 1) * step)
        bins[at, :] = raw[at, :].astype(jnp.float32).astype(jnp.bfloat16)
    hist_body(plan, 0, count, True, bins, spread, keep, send)


def next_kernel(plan, first_unit, count, bins, spread, keep, send):
    hist_body(plan, first_unit, count, False, bins, spread, keep, send)


class Chain:
    def __init__(self):
        self.last = None

    def __call__(
        self, body, out_shape, operands, flops=0, moved=0, in_place=None, out_place=None, **more
    ):
        n = len(operands)
        spec = {
            True: pl.BlockSpec(memory_space=pltpu.VMEM),
            False: pl.BlockSpec(memory_space=pl.ANY),
            None: pl.BlockSpec(memory_space=pltpu.HBM),
        }
        in_specs = [spec[x] for x in in_place or [True] * n]
        out_specs = [spec[x] for x in out_place or [True] * len(out_shape)]
        operands = list(operands)
        if self.last is not None:
            in_specs.append(spec[False])
            operands.append(self.last)

            def run(*refs):
                body(*refs[:n], *refs[n + 1 :])
        else:
            run = body
        outs = pl.pallas_call(
            run,
            out_shape=out_shape,
            in_specs=in_specs,
            out_specs=out_specs,
            compiler_params=pltpu.CompilerParams(vmem_limit_bytes=VMEM_LIMIT),
            cost_estimate=pl.CostEstimate(flops=10**10, bytes_accessed=1024, transcendentals=0),
            **more,
        )(*operands)
        self.last = outs[-1]
        return outs


def f32(*shape):
    return jax.ShapeDtypeStruct(shape, jnp.float32)


def add_body(n_outs, *refs):
    parts, outs = refs[:-n_outs], refs[-n_outs:]
    each = outs[0].shape[0]
    row = 0
    for mine, theirs in zip(parts[::2], parts[1::2], strict=True):
        rows = mine.shape[1]
        for i, out in enumerate(outs):
            at = slice(i * each, (i + 1) * each)
            out[:, row : row + rows, :] = mine[at] + theirs[at]
        row += rows


def join_body(*refs):
    parts, out = refs[:-1], refs[-1]
    each = out.shape[0] // len(parts)
    for i, part in enumerate(parts):
        out[i * each : (i + 1) * each] = part[...]


def score(g, h):
    return g * g / (h + RIDGE)


def curves_body(sizes, n_parts, first_unit, has_totals, last, *refs):
    n = sum(n for n, _ in n_parts)
    parts, refs = refs[:n], refs[n:]
    if has_totals:
        weights, *refs = refs
        if not last:
            totals, gains = refs
    elif last:
        packed, old_gains, weights = refs
    else:
        packed, old_gains, weights, gains = refs
    width = weights.shape[2]
    row = lax.broadcasted_iota(jnp.int32, (EXTRA, width), 0)

    def summed(mine, start):
        total = mine[0][0, start : start + EXTRA, :]
        for part in mine[1:]:
            total += part[0, start : start + EXTRA, :]
        return total

    if has_totals:
        block = summed(parts[: n_parts[0][0]], sizes[0] * 2 * K)
        gain_rows = jnp.zeros((EXTRA, width), jnp.float32)
        if not last:
            totals[...] = block
    else:
        block = packed[...]
        gain_rows = old_gains[...]
    columns = [
        jnp.broadcast_to(block[:, i : i + 1], (EXTRA, width)) for i in range(2 * K // EXTRA)
    ]
    unit = 0
    taken = 0
    for n, chunks in n_parts:
        mine = parts[taken : taken + n]
        taken += n
        at = 0
        for chunk in chunks:
            for u in range(sizes[chunk]):
                gain = jnp.zeros((EXTRA, width), jnp.float32)
                for i in range(K // EXTRA):
                    gl = summed(mine, at + i * EXTRA)
                    hl = summed(mine, at + K + i * EXTRA)
                    g, h = columns[i], columns[K // EXTRA + i]
                    gain += score(gl, hl) + score(g - gl, h - hl) - score(g, h)
                    to = unit * K + i * EXTRA
                    weights[0, to : to + EXTRA, :] = -gl / (hl + RIDGE)
                mean = jnp.sum(gain, axis=0, keepdims=True) / K
                gain_rows = jnp.where(row == first_unit + unit, mean, gain_rows)
                at += 2 * K
                unit += 1
            if has_totals and chunk == 0:
                at += EXTRA
    if last:
        weights[0, unit * K : unit * K + EXTRA, :] = gain_rows
    else:
        gains[...] = gain_rows


def place_body(plan, first_unit, count, last, first, *refs):
    if not first:
        refs = refs[1:]
    mine, theirs, weights = refs[:3]
    if last:
        gains, held, lines, sems, held_sems = refs[3:]
    else:
        token, sems = refs[3:]
        token[...] = jnp.zeros_like(token)
    me = lax.axis_index("dp")
    copies = []
    fetched = []
    for side, source in enumerate((mine, theirs)):
        who = me ^ side
        if last:
            fetch = pltpu.make_async_copy(
                source.at[:, pl.ds(count * K, EXTRA), :], held.at[side], held_sems.at[side]
            )
            fetch.start()
            fetched.append(fetch)
        for item in range(plan.items):
            low_bin = plan.low_bin(who, item)
            for u in range(count):
                copy = pltpu.make_async_copy(
                    source.at[item, pl.ds(u * K, K), :],
                    weights.at[who & 1, (first_unit + u) * plan.unit + low_bin],
                    sems.at[(side * plan.items + item) * count + u],
                )
                copy.start()
                copies.append(copy)
    if last:
        for side in range(2):
            fetched[side].wait()
        for side in range(2):
            who = me ^ side
            for item in range(plan.items):
                low_bin = plan.low_bin(who, item)
                for u in range(plan.units):
                    line = pl.ds(u * plan.unit + low_bin, 1)
                    for h in range(lines.shape[0]):
                        lines[h, who & 1, line, :] = held[
                            side, item, u : u + 1, h * LANES : (h + 1) * LANES
                        ]
        for h in range(lines.shape[0]):
            gains[:, :, h * LANES : (h + 1) * LANES] = lines[h]
    for copy in copies:
        copy.wait()


def on_device(bin_index, node_ids, gradients, hessians):
    devices = lax.axis_size("dp")
    plan = Plan(devices)
    rows, features = bin_index.shape
    width = gradients.shape[1]
    chain = Chain()

    def swap(x, partner):
        return lax.ppermute(x, "dp", [(d, partner(d)) for d in range(devices)])

    def swap_stage(x, stage):
        return swap(x, functools.partial(plan.partner, stage))

    def swap_cores(x):
        return swap(x, lambda d: d ^ 1)

    def swap_top(x):
        return swap(x, lambda d: d ^ plan.top)

    sizes, bundles, batches = plan.sizes()
    starts = [sum(sizes[:i]) for i in range(len(sizes))]
    n_stages = len(plan.stages)
    got = {}
    shared = {}

    def depth(chunk):
        return sizes[chunk] * 2 * K + (EXTRA if chunk == 0 else 0)

    def add(parts, groups):
        height = sum(p.shape[1] for p, _ in parts)
        items = parts[0][0].shape[0] // groups
        return chain(
            functools.partial(add_body, groups), [f32(items, height, features)] * groups, sum(parts, [])
        )

    def histogram(c):
        halves = [f32(plan.items, depth(c), features)] * 2
        if c == 0:
            blocks = 8
            keep, send, bins, spread = chain(
                functools.partial(first_kernel, plan, sizes[c], blocks),
                [
                    *halves,
                    jax.ShapeDtypeStruct((rows, features), jnp.bfloat16),
                    jax.ShapeDtypeStruct((NODES * 2 * K, rows), jnp.bfloat16),
                ],
                [
                    pltpu.with_memory_space_constraint(x, pltpu.HBM)
                    for x in (bin_index, node_ids.reshape(1, rows), gradients.T, hessians.T)
                ],
                in_place=[None] * 4,
                scratch_shapes=[
                    pltpu.VMEM((rows, features), jnp.int32),
                    pltpu.VMEM((1, rows), jnp.int32),
                    pltpu.VMEM((2 * width, rows), jnp.bfloat16),
                    pltpu.SemaphoreType.DMA((3 + blocks,)),
                ],
            )
            shared["data"] = (bins, spread)
        else:
            keep, send = chain(
                functools.partial(next_kernel, plan, starts[c], sizes[c]), halves, shared["data"]
            )
        got["C", c] = [keep, swap_cores(send)]

    def over_cores(c):
        mine, other = add([got["C", c]], 2)
        got["S", c] = [mine, swap_stage(other, 0)]

    def over_first(c):
        mine, other = add([got["S", c]], 2)
        got["T", c] = [mine, swap_stage(other, 1)]

    def over_next(b, stage):
        parts = [got["T", c] for c in bundles[b]] if stage == 2 else [got["Z", b]]
        if stage < n_stages:
            mine, other = add(parts, 2)
            got["Z", b] = [mine, swap_stage(other, stage)]
        else:
            (mine,) = add(parts, 1)
            got["Z", b] = [mine, swap_top(mine)]

    def curves(g):
        batch = batches[g]
        chunks = [c for b in batch for c in bundles[b]]
        count = sum(sizes[c] for c in chunks)
        last = g == len(batches) - 1
        parts = sum((got["Z", b] for b in batch), [])
        n_parts = [(len(got["Z", b]), bundles[b]) for b in batch]
        outs = [f32(1, count * K + (EXTRA if last else 0), features)]
        if not last:
            outs += [f32(EXTRA, features)] * (2 if g == 0 else 1)
        extra = [] if g == 0 else [shared["totals"], shared["gains"]]
        outs = chain(
            functools.partial(curves_body, sizes, n_parts, starts[chunks[0]], g == 0, last),
            outs,
            parts + extra,
        )
        if not last:
            shared["gains"] = outs[-1]
            if g == 0:
                shared["totals"] = outs[1]
        got["G", g] = [outs[0], swap_stage(outs[0], n_stages - 1)]

    def gather(g, stage):
        parts = got["G", g]
        items, height, _ = parts[0].shape
        (joined,) = chain(join_body, [f32(2 * items, height, features)], parts)
        got["G", g] = [joined, swap_stage(joined, stage - 1) if stage else swap_cores(joined)]

    def place(g):
        chunks = [c for b in batches[g] for c in bundles[b]]
        count = sum(sizes[c] for c in chunks)
        last = g == len(batches) - 1
        out_shape = [f32(NODES, B, K, features), f32(EXTRA, LANES)]
        scratch = [pltpu.SemaphoreType.DMA((2 * plan.items * count,))]
        if last:
            out_shape[1] = f32(NODES, B, features)
            scratch = [
                pltpu.VMEM((2, plan.items, EXTRA, features), jnp.float32),
                pltpu.VMEM((features // LANES, NODES, B, LANES), jnp.float32),
                *scratch,
                pltpu.SemaphoreType.DMA((2,)),
            ]
        buffer = [] if g == 0 else [shared["weights"]]
        operands = [*buffer, *got["G", g]]
        shared["weights"], shared["gains_out"] = chain(
            functools.partial(place_body, plan, starts[chunks[0]], count, last, g == 0),
            out_shape,
            operands,
            in_place=[None] * len(buffer) + [False] * 2,
            out_place=[None, True],
            scratch_shapes=scratch,
            input_output_aliases={0: 0} if buffer else {},
        )

    tasks = []
    for c in range(len(sizes)):
        tasks += [(c - 0.2, histogram, c), (c + 0.9, over_cores, c), (c + 2, over_first, c)]
    for b, bundle in enumerate(bundles):
        for stage in range(2, n_stages + 1):
            tasks.append((bundle[-1] + 1 + stage + 0.02 * stage, over_next, b, stage))
    for g, batch in enumerate(batches):
        at = bundles[batch[-1]][-1] + n_stages + 2.1 - (0.5 if g < len(batches) - 1 else 0)
        tasks.append((at, curves, g))
        for i, stage in enumerate(reversed(range(n_stages))):
            tasks.append((at + 1 + i, gather, g, stage))
        tasks.append((at + 1 + n_stages, place, g))
    for _, task, *arguments in sorted(tasks, key=lambda t: t[0]):
        task(*arguments)
    return shared["gains_out"].transpose(2, 0, 1), shared["weights"].transpose(3, 0, 1, 2)


def solution(mesh):
    return jax.shard_map(
        on_device,
        mesh=mesh,
        in_specs=(P("dp", None), P("dp"), P("dp", None), P("dp", None)),
        out_specs=(P(), P()),
        check_vma=False,
    )
```

```python
import functools

import jax
import jax.numpy as jnp
from jax import lax
from jax.experimental import pallas as pl
from jax.experimental.pallas import tpu as pltpu
from jax.sharding import PartitionSpec as P

B = 64
K = 32
NODES = 2
RIDGE = 1.0
LANES = 128
EXTRA = 8
VMEM_LIMIT = 48 * 2**20
SIZES = [2, 2, 2, 2]
BATCHES = [[0], [1], [2], [3]]
HALVE = [('xyz', 'yxz'), ('zxy', 'xyz'), ('zxy', 'yzx'), ('xzy', 'yxz')]
GATHER = [('xyz', 'zxy'), ('xzy', 'yzx'), ('xzy', 'zyx'), ('xzy', 'zyx')]
ORDER = [('K', 0), ('K', 1), ('S', 0, 0), ('S', 1, 0), ('K', 2), ('S', 0, 1), ('S', 2, 0), ('K', 3), ('S', 1, 1), ('S', 0, 2), ('S', 3, 0), ('S', 2, 1), ('S', 1, 2), ('S', 0, 3), ('S', 3, 1), ('S', 1, 3), ('S', 2, 2), ('S', 3, 2), ('S', 2, 3), ('R', 0), ('S', 3, 3), ('R', 1), ('G', 0, 2), ('G', 1, 2), ('R', 2), ('G', 0, 1), ('G', 2, 2), ('R', 3), ('G', 1, 1), ('G', 3, 2), ('G', 2, 1), ('G', 1, 0), ('G', 3, 1), ('G', 0, 0), ('G', 2, 0), ('P', 0), ('P', 1), ('G', 3, 0), ('P', 2), ('P', 3)]
FLIP = {"x": 2, "y": 4, "z": 8}


class Plan:
    def __init__(self, devices):
        bits = devices.bit_length() - 1
        assert devices == 1 << bits and bits >= 4
        self.top = devices // 2
        self.unit = self.items = devices // 4
        self.units = B // self.unit
        assert self.units >= 1
        self.n_stages = bits - 2
        if devices == 32 and self.units == sum(SIZES):
            self.sizes, self.batches, self.order = SIZES, BATCHES, ORDER
            self.halve = [self.paths(*pair) for pair in HALVE]
            self.gather = [self.paths(*pair) for pair in GATHER]
        else:
            self.sizes, self.batches, self.order = [self.units], [[0]], []
            later = [(1 << b, 1 << b) for b in range(3, bits - 1)]
            self.halve = self.gather = [[(2, 4), (4, 2), *later]]

    def paths(self, even, odd):
        return [(FLIP[e], FLIP[o]) for e, o in zip(even, odd, strict=True)]


def mask(path, item, core):
    total = 0
    for i, (even, odd) in enumerate(reversed(path)):
        total = total ^ (((item >> i) & 1) * (even + core * (odd - even)))
    return total


def low_bin(path, device, item):
    return ((device ^ mask(path, item, device & 1)) >> 1) & ((1 << len(path)) - 1)


def mirrored(path, item, core):
    even, odd = ([stage[c] for stage in reversed(path)] for c in (0, 1))
    total = 0
    for i in range(len(path)):
        on_even, on_odd = 1 << odd.index(even[i]), 1 << even.index(odd[i])
        total = total ^ (((item >> i) & 1) * (on_even + core * (on_odd - on_even)))
    return total


def hist_body(plan, path, first_unit, count, has_totals, bins, spread, keep, send):
    me = lax.axis_index("dp")
    rows = bins.shape[0]
    step = min(rows, 256)

    @pl.loop(0, plan.items)
    def _(item):
        own = low_bin(path, me, item)
        theirs = mirrored(path, item, me & 1)
        for u in range(count):
            level = (first_unit + u) * plan.unit + own
            level = level.astype(jnp.float32).astype(jnp.bfloat16)
            total = jnp.zeros((spread.shape[0], bins.shape[1]), jnp.float32)
            for start in range(0, rows, step):
                below = jnp.where(
                    bins[start : start + step, :] <= level, jnp.bfloat16(1), jnp.bfloat16(0)
                )
                total += jnp.dot(
                    spread[:, start : start + step], below, preferred_element_type=jnp.float32
                )
            at = pl.ds(u * 2 * K, 2 * K)
            keep[item, at, :] = total[: 2 * K, :]
            send[theirs, at, :] = total[2 * K :, :]

    if has_totals:
        sums = jnp.sum(spread[...].astype(jnp.float32), axis=1, keepdims=True)
        lane = lax.broadcasted_iota(jnp.int32, (EXTRA, bins.shape[1]), 1)
        for target, base in ((keep, 0), (send, 2 * K)):
            packed = jnp.zeros((EXTRA, bins.shape[1]), jnp.float32)
            for i in range(2 * K // EXTRA):
                part = sums[base + i * EXTRA : base + (i + 1) * EXTRA, :]
                packed = jnp.where(lane == i, part, packed)
            for item in range(plan.items):
                target[item, pl.ds(count * 2 * K, EXTRA), :] = packed


def first_kernel(plan, path, count, blocks, *refs):
    bins_in, node_in, grad_in, hess_in, keep, send, bins, spread = refs[:8]
    raw, node, paired, sems = refs[8:]
    me = lax.axis_index("dp")
    core = me & 1
    step = bins.shape[0] // blocks
    width = grad_in.shape[0]
    small = [
        pltpu.make_async_copy(node_in, node, sems.at[0]),
        pltpu.make_async_copy(grad_in, paired.at[pl.ds(0, width), :], sems.at[1]),
        pltpu.make_async_copy(hess_in, paired.at[pl.ds(width, width), :], sems.at[2]),
    ]
    large = [
        pltpu.make_async_copy(
            bins_in.at[pl.ds(i * step, step), :], raw.at[pl.ds(i * step, step), :], sems.at[3 + i]
        )
        for i in range(blocks)
    ]
    for copy in small + large:
        copy.start()
    for copy in small:
        copy.wait()
    for slot in range(NODES):
        here = (node[...] == (core ^ slot)).astype(jnp.float32)
        spread[slot * 2 * K : (slot + 1) * 2 * K, :] = (
            paired[...].astype(jnp.float32) * here
        ).astype(jnp.bfloat16)
    for i, copy in enumerate(large):
        copy.wait()
        at = slice(i * step, (i + 1) * step)
        bins[at, :] = raw[at, :].astype(jnp.float32).astype(jnp.bfloat16)
    hist_body(plan, path, 0, count, True, bins, spread, keep, send)


def next_kernel(plan, path, first_unit, count, bins, spread, keep, send):
    hist_body(plan, path, first_unit, count, False, bins, spread, keep, send)


class Chain:
    def __init__(self):
        self.last = None

    def __call__(
        self, body, out_shape, operands, flops=10**10, in_place=None, out_place=None, **more
    ):
        n = len(operands)
        spec = {
            True: pl.BlockSpec(memory_space=pltpu.VMEM),
            False: pl.BlockSpec(memory_space=pl.ANY),
            None: pl.BlockSpec(memory_space=pltpu.HBM),
        }
        in_specs = [spec[x] for x in in_place or [True] * n]
        out_specs = [spec[x] for x in out_place or [True] * len(out_shape)]
        operands = list(operands)
        if self.last is not None:
            in_specs.append(spec[False])
            operands.append(self.last)

            def run(*refs):
                body(*refs[:n], *refs[n + 1 :])
        else:
            run = body
        outs = pl.pallas_call(
            run,
            out_shape=out_shape,
            in_specs=in_specs,
            out_specs=out_specs,
            compiler_params=pltpu.CompilerParams(vmem_limit_bytes=VMEM_LIMIT),
            cost_estimate=pl.CostEstimate(flops=flops, bytes_accessed=1024, transcendentals=0),
            **more,
        )(*operands)
        self.last = outs[-1]
        return outs


def f32(*shape):
    return jax.ShapeDtypeStruct(shape, jnp.float32)


def add_body(n_outs, *refs):
    parts, outs = refs[:-n_outs], refs[-n_outs:]
    each = outs[0].shape[0]
    row = 0
    for mine, theirs in zip(parts[::2], parts[1::2], strict=True):
        rows = mine.shape[1]
        for i, out in enumerate(outs):
            at = slice(i * each, (i + 1) * each)
            out[:, row : row + rows, :] = mine[at] + theirs[at]
        row += rows


def join_body(*refs):
    parts, out = refs[:-1], refs[-1]
    each = out.shape[0] // len(parts)
    for i, part in enumerate(parts):
        out[i * each : (i + 1) * each] = part[...]


def score(g, h):
    return g * g / (h + RIDGE)


def curves_body(sizes, n_parts, first_unit, has_totals, last, *refs):
    n = sum(n for n, _ in n_parts)
    parts, refs = refs[:n], refs[n:]
    if has_totals:
        weights, *refs = refs
        if not last:
            totals, gains = refs
    elif last:
        packed, old_gains, weights = refs
    else:
        packed, old_gains, weights, gains = refs
    width = weights.shape[2]
    row = lax.broadcasted_iota(jnp.int32, (EXTRA, width), 0)

    def summed(mine, start):
        total = mine[0][0, start : start + EXTRA, :]
        for part in mine[1:]:
            total += part[0, start : start + EXTRA, :]
        return total

    if has_totals:
        block = summed(parts[: n_parts[0][0]], sizes[0] * 2 * K)
        gain_rows = jnp.zeros((EXTRA, width), jnp.float32)
        if not last:
            totals[...] = block
    else:
        block = packed[...]
        gain_rows = old_gains[...]
    columns = [
        jnp.broadcast_to(block[:, i : i + 1], (EXTRA, width)) for i in range(2 * K // EXTRA)
    ]
    unit = 0
    taken = 0
    for n, chunks in n_parts:
        mine = parts[taken : taken + n]
        taken += n
        at = 0
        for chunk in chunks:
            for u in range(sizes[chunk]):
                gain = jnp.zeros((EXTRA, width), jnp.float32)
                for i in range(K // EXTRA):
                    gl = summed(mine, at + i * EXTRA)
                    hl = summed(mine, at + K + i * EXTRA)
                    g, h = columns[i], columns[K // EXTRA + i]
                    gain += score(gl, hl) + score(g - gl, h - hl) - score(g, h)
                    to = unit * K + i * EXTRA
                    weights[0, to : to + EXTRA, :] = -gl / (hl + RIDGE)
                mean = jnp.sum(gain, axis=0, keepdims=True) / K
                gain_rows = jnp.where(row == first_unit + unit, mean, gain_rows)
                at += 2 * K
                unit += 1
            if has_totals and chunk == 0:
                at += EXTRA
    if last:
        weights[0, unit * K : unit * K + EXTRA, :] = gain_rows
    else:
        gains[...] = gain_rows


def place_body(plan, path, first_unit, count, last, first, *refs):
    if not first:
        refs = refs[1:]
    mine, theirs, weights = refs[:3]
    if last:
        gains, held, lines, sems, held_sems = refs[3:]
    else:
        token, sems = refs[3:]
        token[...] = jnp.zeros_like(token)
    me = lax.axis_index("dp")
    copies = []
    fetched = []
    for side, source in enumerate((mine, theirs)):
        who = me ^ side
        if last:
            fetch = pltpu.make_async_copy(
                source.at[:, pl.ds(count * K, EXTRA), :], held.at[side], held_sems.at[side]
            )
            fetch.start()
            fetched.append(fetch)
        for item in range(plan.items):
            own = low_bin(path, who, item)
            for u in range(count):
                copy = pltpu.make_async_copy(
                    source.at[item, pl.ds(u * K, K), :],
                    weights.at[who & 1, (first_unit + u) * plan.unit + own],
                    sems.at[(side * plan.items + item) * count + u],
                )
                copy.start()
                copies.append(copy)
    if last:
        for side in range(2):
            fetched[side].wait()
        for side in range(2):
            who = me ^ side
            for item in range(plan.items):
                own = low_bin(path, who, item)
                for u in range(plan.units):
                    line = pl.ds(u * plan.unit + own, 1)
                    for h in range(lines.shape[0]):
                        lines[h, who & 1, line, :] = held[
                            side, item, u : u + 1, h * LANES : (h + 1) * LANES
                        ]
        for h in range(lines.shape[0]):
            gains[:, :, h * LANES : (h + 1) * LANES] = lines[h]
    for copy in copies:
        copy.wait()


def on_device(bin_index, node_ids, gradients, hessians):
    devices = lax.axis_size("dp")
    plan = Plan(devices)
    rows, features = bin_index.shape
    width = gradients.shape[1]
    chain = Chain()

    def swap(x, partner):
        return lax.ppermute(x, "dp", [(d, partner(d)) for d in range(devices)])

    def swap_stage(x, stage):
        return swap(x, lambda d: d ^ stage[d & 1])

    def swap_cores(x):
        return swap(x, lambda d: d ^ 1)

    def swap_top(x):
        return swap(x, lambda d: d ^ plan.top)

    sizes, batches = plan.sizes, plan.batches
    starts = [sum(sizes[:i]) for i in range(len(sizes))]
    n_stages = plan.n_stages
    got = {}
    shared = {}

    def depth(chunk):
        return sizes[chunk] * 2 * K + (EXTRA if chunk == 0 else 0)

    def add(pair, n_outs):
        items, height, _ = pair[0].shape
        return chain(
            functools.partial(add_body, n_outs), [f32(items // n_outs, height, features)] * n_outs, pair
        )

    def histogram(c):
        halves = [f32(plan.items, depth(c), features)] * 2
        if c == 0:
            blocks = 8
            keep, send, bins, spread = chain(
                functools.partial(first_kernel, plan, plan.halve[c], sizes[c], blocks),
                [
                    *halves,
                    jax.ShapeDtypeStruct((rows, features), jnp.bfloat16),
                    jax.ShapeDtypeStruct((NODES * 2 * K, rows), jnp.bfloat16),
                ],
                [
                    pltpu.with_memory_space_constraint(x, pltpu.HBM)
                    for x in (bin_index, node_ids.reshape(1, rows), gradients.T, hessians.T)
                ],
                in_place=[None] * 4,
                scratch_shapes=[
                    pltpu.VMEM((rows, features), jnp.int32),
                    pltpu.VMEM((1, rows), jnp.int32),
                    pltpu.VMEM((2 * width, rows), jnp.bfloat16),
                    pltpu.SemaphoreType.DMA((3 + blocks,)),
                ],
            )
            shared["data"] = (bins, spread)
        else:
            keep, send = chain(
                functools.partial(next_kernel, plan, plan.halve[c], starts[c], sizes[c]),
                halves,
                shared["data"],
                flops=10**10,
            )
        got[c] = [keep, swap_cores(send)]

    def reduce(c, stage):
        if stage < n_stages:
            mine, other = add(got[c], 2)
            got[c] = [mine, swap_stage(other, plan.halve[c][stage])]
        else:
            (mine,) = add(got[c], 1)
            got[c] = [mine, swap_top(mine)]

    def curves(g):
        chunks = batches[g]
        count = sum(sizes[c] for c in chunks)
        last = g == len(batches) - 1
        parts = sum((got[c] for c in chunks), [])
        n_parts = [(2, [c]) for c in chunks]
        outs = [f32(1, count * K + (EXTRA if last else 0), features)]
        if not last:
            outs += [f32(EXTRA, features)] * (2 if g == 0 else 1)
        extra = [] if g == 0 else [shared["totals"], shared["gains"]]
        outs = chain(
            functools.partial(curves_body, sizes, n_parts, starts[chunks[0]], g == 0, last),
            outs,
            parts + extra,
        )
        if not last:
            shared["gains"] = outs[-1]
            if g == 0:
                shared["totals"] = outs[1]
        got["G", g] = [outs[0], swap_stage(outs[0], plan.gather[g][-1])]

    def gather(g, stage):
        parts = got["G", g]
        items, height, _ = parts[0].shape
        (joined,) = chain(join_body, [f32(2 * items, height, features)], parts)
        if stage:
            got["G", g] = [joined, swap_stage(joined, plan.gather[g][stage - 1])]
        else:
            got["G", g] = [joined, swap_cores(joined)]

    def place(g):
        chunks = batches[g]
        count = sum(sizes[c] for c in chunks)
        last = g == len(batches) - 1
        out_shape = [f32(NODES, B, K, features), f32(EXTRA, LANES)]
        scratch = [pltpu.SemaphoreType.DMA((2 * plan.items * count,))]
        if last:
            out_shape[1] = f32(NODES, B, features)
            scratch = [
                pltpu.VMEM((2, plan.items, EXTRA, features), jnp.float32),
                pltpu.VMEM((features // LANES, NODES, B, LANES), jnp.float32),
                *scratch,
                pltpu.SemaphoreType.DMA((2,)),
            ]
        buffer = [] if g == 0 else [shared["weights"]]
        operands = [*buffer, *got["G", g]]
        shared["weights"], shared["gains_out"] = chain(
            functools.partial(place_body, plan, plan.gather[g], starts[chunks[0]], count, last, g == 0),
            out_shape,
            operands,
            in_place=[None] * len(buffer) + [False] * 2,
            out_place=[None, True],
            scratch_shapes=scratch,
            input_output_aliases={0: 0} if buffer else {},
        )

    tasks = []
    for c in range(len(sizes)):
        tasks.append((c - 0.2, ("K", c)))
        for stage in range(n_stages + 1):
            tasks.append((c + 1 + 1.02 * stage, ("S", c, stage)))
    for g, chunks in enumerate(batches):
        at = chunks[-1] + n_stages + 2.1 - (0.5 if g < len(batches) - 1 else 0)
        tasks.append((at, ("R", g)))
        for i, stage in enumerate(reversed(range(n_stages))):
            tasks.append((at + 1 + i, ("G", g, stage)))
        tasks.append((at + 1 + n_stages, ("P", g)))
    kinds = {"K": histogram, "S": reduce, "R": curves, "G": gather, "P": place}
    for name, *arguments in plan.order or [task for _, task in sorted(tasks, key=lambda t: t[0])]:
        kinds[name](*arguments)
    return shared["gains_out"].transpose(2, 0, 1), shared["weights"].transpose(3, 0, 1, 2)


def solution(mesh):
    return jax.shard_map(
        on_device,
        mesh=mesh,
        in_specs=(P("dp", None), P("dp"), P("dp", None), P("dp", None)),
        out_specs=(P(), P()),
        check_vma=False,
    )
```

```python
import functools

import jax
import jax.numpy as jnp
from jax import lax
from jax.experimental import pallas as pl
from jax.experimental.pallas import tpu as pltpu
from jax.sharding import PartitionSpec as P

B = 64
K = 32
NODES = 2
RIDGE = 1.0
LANES = 128
EXTRA = 8
VMEM_LIMIT = 48 * 2**20
SIZES = [1, 1, 2, 2, 2]
BATCHES = [[0, 1], [2], [3], [4]]
HALVE = [('zxy', 'zyx'), ('zxy', 'zyx'), ('xzy', 'yzx'), ('xzy', 'yzx'), ('xyz', 'yxz')]
GATHER = [('xzy', 'yzx'), ('xzy', 'yzx'), ('zxy', 'zyx'), ('xyz', 'yxz')]
ORDER = [('K', 0), ('K', 2), ('S', 0, 0), ('K', 1), ('S', 2, 0), ('K', 3), ('S', 1, 0), ('S', 0, 1), ('S', 3, 0), ('K', 4), ('S', 2, 1), ('S', 1, 1), ('S', 0, 2), ('S', 4, 0), ('S', 0, 3), ('S', 1, 2), ('S', 3, 1), ('S', 2, 2), ('S', 4, 1), ('S', 1, 3), ('S', 2, 3), ('S', 3, 2), ('S', 4, 2), ('R', 0), ('S', 3, 3), ('G', 0, 2), ('R', 1), ('S', 4, 3), ('R', 2), ('G', 1, 2), ('G', 2, 2), ('R', 3), ('G', 0, 1), ('G', 2, 1), ('G', 3, 2), ('G', 1, 1), ('G', 0, 0), ('G', 3, 1), ('G', 1, 0), ('G', 2, 0), ('P', 0), ('P', 1), ('G', 3, 0), ('P', 2), ('P', 3)]
DOTS = 8
FLIP = {"x": 2, "y": 4, "z": 8}


class Plan:
    def __init__(self, devices):
        bits = devices.bit_length() - 1
        assert devices == 1 << bits and bits >= 4
        self.top = devices // 2
        self.unit = self.items = devices // 4
        self.units = B // self.unit
        assert 1 <= self.units <= EXTRA
        self.n_stages = bits - 2
        if devices == 32 and self.units == sum(SIZES):
            self.sizes, self.batches, self.order = SIZES, BATCHES, ORDER
            self.halve = [self.paths(*pair) for pair in HALVE]
            self.gather = [self.paths(*pair) for pair in GATHER]
        else:
            self.sizes, self.batches, self.order = [self.units], [[0]], []
            later = [(1 << b, 1 << b) for b in range(3, bits - 1)]
            self.halve = self.gather = [[(2, 4), (4, 2), *later]]

    def paths(self, even, odd):
        return [(FLIP[e], FLIP[o]) for e, o in zip(even, odd, strict=True)]


def mask(path, item, core):
    total = 0
    for i, (even, odd) in enumerate(reversed(path)):
        total = total ^ (((item >> i) & 1) * (even + core * (odd - even)))
    return total


def low_bin(path, device, item):
    return ((device ^ mask(path, item, device & 1)) >> 1) & ((1 << len(path)) - 1)


def mirrored(path, item, core):
    even, odd = ([stage[c] for stage in reversed(path)] for c in (0, 1))
    total = 0
    for i in range(len(path)):
        on_even, on_odd = 1 << odd.index(even[i]), 1 << even.index(odd[i])
        total = total ^ (((item >> i) & 1) * (on_even + core * (on_odd - on_even)))
    return total


def hist_body(plan, path, first_unit, count, has_totals, bins, spread, keep, send):
    me = lax.axis_index("dp")
    rows = bins.shape[0]
    step = min(rows, 256)

    def one(item):
        own = low_bin(path, me, item)
        theirs = mirrored(path, item, me & 1)
        for u in range(count):
            level = (first_unit + u) * plan.unit + own
            level = level.astype(jnp.float32).astype(jnp.bfloat16)
            total = jnp.zeros((spread.shape[0], bins.shape[1]), jnp.float32)
            for start in range(0, rows, step):
                below = jnp.where(
                    bins[start : start + step, :] <= level, jnp.bfloat16(1), jnp.bfloat16(0)
                )
                total += jnp.dot(
                    spread[:, start : start + step], below, preferred_element_type=jnp.float32
                )
            at = pl.ds(u * 2 * K, 2 * K)
            keep[item, at, :] = total[: 2 * K, :]
            send[theirs, at, :] = total[2 * K :, :]

    together = max(1, DOTS // count)

    @pl.loop(0, plan.items // together)
    def _(turn):
        for i in range(together):
            one(turn * together + i)

    if has_totals:
        sums = jnp.sum(spread[...].astype(jnp.float32), axis=1, keepdims=True)
        lane = lax.broadcasted_iota(jnp.int32, (EXTRA, bins.shape[1]), 1)
        for target, base in ((keep, 0), (send, 2 * K)):
            packed = jnp.zeros((EXTRA, bins.shape[1]), jnp.float32)
            for i in range(2 * K // EXTRA):
                part = sums[base + i * EXTRA : base + (i + 1) * EXTRA, :]
                packed = jnp.where(lane == i, part, packed)
            for item in range(plan.items):
                target[item, pl.ds(count * 2 * K, EXTRA), :] = packed


def first_kernel(plan, path, count, blocks, *refs):
    bins_in, node_in, grad_in, hess_in, keep, send, bins, spread = refs[:8]
    raw, node, paired, sems = refs[8:]
    me = lax.axis_index("dp")
    core = me & 1
    step = bins.shape[0] // blocks
    width = grad_in.shape[0]
    small = [
        pltpu.make_async_copy(node_in, node, sems.at[0]),
        pltpu.make_async_copy(grad_in, paired.at[pl.ds(0, width), :], sems.at[1]),
        pltpu.make_async_copy(hess_in, paired.at[pl.ds(width, width), :], sems.at[2]),
    ]
    large = [
        pltpu.make_async_copy(
            bins_in.at[pl.ds(i * step, step), :], raw.at[pl.ds(i * step, step), :], sems.at[3 + i]
        )
        for i in range(blocks)
    ]
    for copy in small + large:
        copy.start()
    for copy in small:
        copy.wait()
    for slot in range(NODES):
        here = (node[...] == (core ^ slot)).astype(jnp.float32)
        spread[slot * 2 * K : (slot + 1) * 2 * K, :] = (
            paired[...].astype(jnp.float32) * here
        ).astype(jnp.bfloat16)
    for i, copy in enumerate(large):
        copy.wait()
        at = slice(i * step, (i + 1) * step)
        bins[at, :] = raw[at, :].astype(jnp.float32).astype(jnp.bfloat16)
    hist_body(plan, path, 0, count, True, bins, spread, keep, send)


def next_kernel(plan, path, first_unit, count, bins, spread, keep, send):
    hist_body(plan, path, first_unit, count, False, bins, spread, keep, send)


class Chain:
    def __init__(self):
        self.last = None

    def __call__(
        self, body, out_shape, operands, flops=10**10, in_place=None, out_place=None, **more
    ):
        n = len(operands)
        spec = {
            True: pl.BlockSpec(memory_space=pltpu.VMEM),
            False: pl.BlockSpec(memory_space=pl.ANY),
            None: pl.BlockSpec(memory_space=pltpu.HBM),
        }
        in_specs = [spec[x] for x in in_place or [True] * n]
        out_specs = [spec[x] for x in out_place or [True] * len(out_shape)]
        operands = list(operands)
        if self.last is not None:
            in_specs.append(spec[False])
            operands.append(self.last)

            def run(*refs):
                body(*refs[:n], *refs[n + 1 :])
        else:
            run = body
        outs = pl.pallas_call(
            run,
            out_shape=out_shape,
            in_specs=in_specs,
            out_specs=out_specs,
            compiler_params=pltpu.CompilerParams(vmem_limit_bytes=VMEM_LIMIT),
            cost_estimate=pl.CostEstimate(flops=flops, bytes_accessed=1024, transcendentals=0),
            **more,
        )(*operands)
        self.last = outs[-1]
        return outs


def f32(*shape):
    return jax.ShapeDtypeStruct(shape, jnp.float32)


def add_body(n_outs, *refs):
    parts, outs = refs[:-n_outs], refs[-n_outs:]
    each = outs[0].shape[0]
    row = 0
    for mine, theirs in zip(parts[::2], parts[1::2], strict=True):
        rows = mine.shape[1]
        for i, out in enumerate(outs):
            at = slice(i * each, (i + 1) * each)
            out[:, row : row + rows, :] = mine[at] + theirs[at]
        row += rows


def join_body(*refs):
    parts, out = refs[:-1], refs[-1]
    each = out.shape[0] // len(parts)
    for i, part in enumerate(parts):
        out[i * each : (i + 1) * each] = part[...]


def score(g, h):
    return g * g / (h + RIDGE)


def curves_body(sizes, n_parts, first_unit, has_totals, last, *refs):
    n = sum(n for n, _ in n_parts)
    parts, refs = refs[:n], refs[n:]
    if has_totals:
        weights, *refs = refs
        if not last:
            totals, gains = refs
    elif last:
        packed, old_gains, weights = refs
    else:
        packed, old_gains, weights, gains = refs
    width = weights.shape[2]
    row = lax.broadcasted_iota(jnp.int32, (EXTRA, width), 0)

    def summed(mine, start):
        total = mine[0][0, start : start + EXTRA, :]
        for part in mine[1:]:
            total += part[0, start : start + EXTRA, :]
        return total

    if has_totals:
        block = summed(parts[: n_parts[0][0]], sizes[0] * 2 * K)
        gain_rows = jnp.zeros((EXTRA, width), jnp.float32)
        if not last:
            totals[...] = block
    else:
        block = packed[...]
        gain_rows = old_gains[...]
    columns = [
        jnp.broadcast_to(block[:, i : i + 1], (EXTRA, width)) for i in range(2 * K // EXTRA)
    ]
    unit = 0
    taken = 0
    for n, chunks in n_parts:
        mine = parts[taken : taken + n]
        taken += n
        at = 0
        for chunk in chunks:
            for u in range(sizes[chunk]):
                gain = jnp.zeros((EXTRA, width), jnp.float32)
                for i in range(K // EXTRA):
                    gl = summed(mine, at + i * EXTRA)
                    hl = summed(mine, at + K + i * EXTRA)
                    g, h = columns[i], columns[K // EXTRA + i]
                    gain += score(gl, hl) + score(g - gl, h - hl) - score(g, h)
                    to = unit * K + i * EXTRA
                    weights[0, to : to + EXTRA, :] = -gl / (hl + RIDGE)
                mean = jnp.sum(gain, axis=0, keepdims=True) / K
                gain_rows = jnp.where(row == first_unit + unit, mean, gain_rows)
                at += 2 * K
                unit += 1
            if has_totals and chunk == 0:
                at += EXTRA
    if last:
        weights[0, unit * K : unit * K + EXTRA, :] = gain_rows
    else:
        gains[...] = gain_rows


def place_body(plan, path, first_unit, count, last, first, *refs):
    if not first:
        refs = refs[1:]
    mine, theirs, weights = refs[:3]
    if last:
        gains, held, lines, sems, held_sems = refs[3:]
    else:
        token, sems = refs[3:]
        token[...] = jnp.zeros_like(token)
    me = lax.axis_index("dp")
    copies = []
    fetched = []
    for side, source in enumerate((mine, theirs)):
        who = me ^ side
        if last:
            fetch = pltpu.make_async_copy(
                source.at[:, pl.ds(count * K, EXTRA), :], held.at[side], held_sems.at[side]
            )
            fetch.start()
            fetched.append(fetch)
        for item in range(plan.items):
            own = low_bin(path, who, item)
            copy = pltpu.make_async_copy(
                source.at[item, pl.ds(0, count * K), :].reshape(count, K, source.shape[2]),
                weights.at[who & 1, pl.ds(first_unit, count), own],
                sems.at[side * plan.items + item],
            )
            copy.start()
            copies.append(copy)
    if last:
        for side in range(2):
            fetched[side].wait()
        for side in range(2):
            who = me ^ side
            for item in range(plan.items):
                own = low_bin(path, who, item)
                for h in range(lines.shape[0]):
                    lines[h, who & 1, own] = held[side, item, :, h * LANES : (h + 1) * LANES]
        for h in range(lines.shape[0]):
            for node in range(NODES):
                for u in range(plan.units):
                    gains[node, u * plan.unit : (u + 1) * plan.unit, h * LANES : (h + 1) * LANES] = lines[
                        h, node, :, u, :
                    ]
    for copy in copies:
        copy.wait()


def on_device(bin_index, node_ids, gradients, hessians):
    devices = lax.axis_size("dp")
    plan = Plan(devices)
    rows, features = bin_index.shape
    width = gradients.shape[1]
    chain = Chain()

    def swap(x, partner):
        return lax.ppermute(x, "dp", [(d, partner(d)) for d in range(devices)])

    def swap_stage(x, stage):
        return swap(x, lambda d: d ^ stage[d & 1])

    def swap_cores(x):
        return swap(x, lambda d: d ^ 1)

    def swap_top(x):
        return swap(x, lambda d: d ^ plan.top)

    sizes, batches = plan.sizes, plan.batches
    starts = [sum(sizes[:i]) for i in range(len(sizes))]
    n_stages = plan.n_stages
    got = {}
    shared = {}

    def depth(chunk):
        return sizes[chunk] * 2 * K + (EXTRA if chunk == 0 else 0)

    def add(pair, n_outs):
        items, height, _ = pair[0].shape
        return chain(
            functools.partial(add_body, n_outs), [f32(items // n_outs, height, features)] * n_outs, pair
        )

    def histogram(c):
        halves = [f32(plan.items, depth(c), features)] * 2
        if c == 0:
            blocks = 8
            keep, send, bins, spread = chain(
                functools.partial(first_kernel, plan, plan.halve[c], sizes[c], blocks),
                [
                    *halves,
                    jax.ShapeDtypeStruct((rows, features), jnp.bfloat16),
                    jax.ShapeDtypeStruct((NODES * 2 * K, rows), jnp.bfloat16),
                ],
                [
                    pltpu.with_memory_space_constraint(x, pltpu.HBM)
                    for x in (bin_index, node_ids.reshape(1, rows), gradients.T, hessians.T)
                ],
                in_place=[None] * 4,
                scratch_shapes=[
                    pltpu.VMEM((rows, features), jnp.int32),
                    pltpu.VMEM((1, rows), jnp.int32),
                    pltpu.VMEM((2 * width, rows), jnp.bfloat16),
                    pltpu.SemaphoreType.DMA((3 + blocks,)),
                ],
            )
            shared["data"] = (bins, spread)
        else:
            keep, send = chain(
                functools.partial(next_kernel, plan, plan.halve[c], starts[c], sizes[c]),
                halves,
                shared["data"],
                flops=10**10,
            )
        got[c] = [keep, swap_cores(send)]

    def reduce(c, stage):
        if stage < n_stages:
            mine, other = add(got[c], 2)
            got[c] = [mine, swap_stage(other, plan.halve[c][stage])]
        else:
            (mine,) = add(got[c], 1)
            got[c] = [mine, swap_top(mine)]

    def curves(g):
        chunks = batches[g]
        count = sum(sizes[c] for c in chunks)
        last = g == len(batches) - 1
        parts = sum((got[c] for c in chunks), [])
        n_parts = [(2, [c]) for c in chunks]
        outs = [f32(1, count * K + (EXTRA if last else 0), features)]
        if not last:
            outs += [f32(EXTRA, features)] * (2 if g == 0 else 1)
        extra = [] if g == 0 else [shared["totals"], shared["gains"]]
        outs = chain(
            functools.partial(curves_body, sizes, n_parts, starts[chunks[0]], g == 0, last),
            outs,
            parts + extra,
        )
        if not last:
            shared["gains"] = outs[-1]
            if g == 0:
                shared["totals"] = outs[1]
        got["G", g] = [outs[0], swap_stage(outs[0], plan.gather[g][-1])]

    def gather(g, stage):
        parts = got["G", g]
        items, height, _ = parts[0].shape
        (joined,) = chain(join_body, [f32(2 * items, height, features)], parts)
        if stage:
            got["G", g] = [joined, swap_stage(joined, plan.gather[g][stage - 1])]
        else:
            got["G", g] = [joined, swap_cores(joined)]

    def place(g):
        chunks = batches[g]
        count = sum(sizes[c] for c in chunks)
        last = g == len(batches) - 1
        out_shape = [f32(NODES, plan.units, plan.unit, K, features), f32(EXTRA, LANES)]
        scratch = [pltpu.SemaphoreType.DMA((2 * plan.items,))]
        if last:
            out_shape[1] = f32(NODES, B, features)
            scratch = [
                pltpu.VMEM((2, plan.items, EXTRA, features), jnp.float32),
                pltpu.VMEM((features // LANES, NODES, plan.unit, EXTRA, LANES), jnp.float32),
                *scratch,
                pltpu.SemaphoreType.DMA((2,)),
            ]
        buffer = [] if g == 0 else [shared["weights"]]
        operands = [*buffer, *got["G", g]]
        shared["weights"], shared["gains_out"] = chain(
            functools.partial(place_body, plan, plan.gather[g], starts[chunks[0]], count, last, g == 0),
            out_shape,
            operands,
            in_place=[None] * len(buffer) + [False] * 2,
            out_place=[None, True],
            scratch_shapes=scratch,
            input_output_aliases={0: 0} if buffer else {},
        )

    tasks = []
    for c in range(len(sizes)):
        tasks.append((c - 0.2, ("K", c)))
        for stage in range(n_stages + 1):
            tasks.append((c + 1 + 1.02 * stage, ("S", c, stage)))
    for g, chunks in enumerate(batches):
        at = chunks[-1] + n_stages + 2.1 - (0.5 if g < len(batches) - 1 else 0)
        tasks.append((at, ("R", g)))
        for i, stage in enumerate(reversed(range(n_stages))):
            tasks.append((at + 1 + i, ("G", g, stage)))
        tasks.append((at + 1 + n_stages, ("P", g)))
    kinds = {"K": histogram, "S": reduce, "R": curves, "G": gather, "P": place}
    for name, *arguments in plan.order or [task for _, task in sorted(tasks, key=lambda t: t[0])]:
        kinds[name](*arguments)
    weights = shared["weights"].reshape(NODES, B, K, features)
    return shared["gains_out"].transpose(2, 0, 1), weights.transpose(3, 0, 1, 2)


def solution(mesh):
    return jax.shard_map(
        on_device,
        mesh=mesh,
        in_specs=(P("dp", None), P("dp"), P("dp", None), P("dp", None)),
        out_specs=(P(), P()),
        check_vma=False,
    )
```

```python
import functools

import jax
import jax.numpy as jnp
from jax import lax
from jax.experimental import pallas as pl
from jax.experimental.pallas import tpu as pltpu
from jax.sharding import PartitionSpec as P

B = 64
K = 32
NODES = 2
RIDGE = 1.0
LANES = 128
EXTRA = 8
VMEM_LIMIT = 48 * 2**20
SIZES = [1, 1, 2, 2, 2]
BATCHES = [[0, 1], [2], [3], [4]]
HALVE = [('zxy', 'zyx'), ('zxy', 'zyx'), ('xzy', 'yzx'), ('xzy', 'yzx'), ('xyz', 'yxz')]
GATHER = [('xzy', 'yzx'), ('xzy', 'yzx'), ('zxy', 'zyx'), ('xyz', 'yxz')]
ORDER = [('K', 0), ('K', 2), ('S', 0, 0), ('K', 1), ('S', 2, 0), ('K', 3), ('S', 1, 0), ('S', 0, 1), ('S', 3, 0), ('K', 4), ('S', 2, 1), ('S', 1, 1), ('S', 0, 2), ('S', 4, 0), ('S', 3, 1), ('S', 0, 3), ('S', 1, 2), ('S', 2, 2), ('S', 4, 1), ('S', 1, 3), ('S', 2, 3), ('S', 3, 2), ('S', 4, 2), ('R', 0), ('S', 3, 3), ('G', 0, 2), ('R', 1), ('S', 4, 3), ('R', 2), ('G', 1, 2), ('G', 2, 2), ('R', 3), ('G', 0, 1), ('G', 2, 1), ('G', 3, 2), ('G', 1, 1), ('G', 0, 0), ('G', 3, 1), ('G', 1, 0), ('G', 2, 0), ('P', 0), ('P', 1), ('G', 3, 0), ('P', 2), ('P', 3)]
DOTS = 8
FLIP = {"x": 2, "y": 4, "z": 8}


class Plan:
    def __init__(self, devices):
        bits = devices.bit_length() - 1
        assert devices == 1 << bits and bits >= 4
        self.top = devices // 2
        self.unit = self.items = devices // 4
        self.units = B // self.unit
        assert 1 <= self.units <= EXTRA
        self.n_stages = bits - 2
        if devices == 32 and self.units == sum(SIZES):
            self.sizes, self.batches, self.order = SIZES, BATCHES, ORDER
            self.halve = [self.paths(*pair) for pair in HALVE]
            self.gather = [self.paths(*pair) for pair in GATHER]
        else:
            self.sizes, self.batches, self.order = [self.units], [[0]], []
            later = [(1 << b, 1 << b) for b in range(3, bits - 1)]
            self.halve = self.gather = [[(2, 4), (4, 2), *later]]

    def paths(self, even, odd):
        return [(FLIP[e], FLIP[o]) for e, o in zip(even, odd, strict=True)]


def mask(path, item, core):
    total = 0
    for i, (even, odd) in enumerate(reversed(path)):
        total = total ^ (((item >> i) & 1) * (even + core * (odd - even)))
    return total


def low_bin(path, device, item):
    return ((device ^ mask(path, item, device & 1)) >> 1) & ((1 << len(path)) - 1)


def mirrored(path, item, core):
    even, odd = ([stage[c] for stage in reversed(path)] for c in (0, 1))
    total = 0
    for i in range(len(path)):
        on_even, on_odd = 1 << odd.index(even[i]), 1 << even.index(odd[i])
        total = total ^ (((item >> i) & 1) * (on_even + core * (on_odd - on_even)))
    return total


def hist_body(plan, path, first_unit, count, has_totals, bins, spread, keep, send):
    me = lax.axis_index("dp")
    rows = bins.shape[0]
    step = min(rows, 256)

    def one(item):
        own = low_bin(path, me, item)
        theirs = mirrored(path, item, me & 1)
        for u in range(count):
            level = (first_unit + u) * plan.unit + own
            level = level.astype(jnp.float32).astype(jnp.bfloat16)
            total = jnp.zeros((spread.shape[0], bins.shape[1]), jnp.float32)
            for start in range(0, rows, step):
                below = jnp.where(
                    bins[start : start + step, :] <= level, jnp.bfloat16(1), jnp.bfloat16(0)
                )
                total += jnp.dot(
                    spread[:, start : start + step], below, preferred_element_type=jnp.float32
                )
            at = pl.ds(u * 2 * K, 2 * K)
            keep[item, at, :] = total[: 2 * K, :]
            send[theirs, at, :] = total[2 * K :, :]

    together = min(plan.items, max(1, DOTS // count))

    @pl.loop(0, plan.items // together)
    def _(turn):
        for i in range(together):
            one(turn * together + i)

    if has_totals:
        sums = jnp.sum(spread[...].astype(jnp.float32), axis=1, keepdims=True)
        lane = lax.broadcasted_iota(jnp.int32, (EXTRA, bins.shape[1]), 1)
        for target, base in ((keep, 0), (send, 2 * K)):
            packed = jnp.zeros((EXTRA, bins.shape[1]), jnp.float32)
            for i in range(2 * K // EXTRA):
                part = sums[base + i * EXTRA : base + (i + 1) * EXTRA, :]
                packed = jnp.where(lane == i, part, packed)
            for item in range(plan.items):
                target[item, pl.ds(count * 2 * K, EXTRA), :] = packed


def first_kernel(plan, path, count, blocks, *refs):
    bins_in, node_in, grad_in, hess_in, keep, send, bins, spread = refs[:8]
    raw, node, paired, sems = refs[8:]
    me = lax.axis_index("dp")
    core = me & 1
    step = bins.shape[0] // blocks
    width = grad_in.shape[0]
    small = [
        pltpu.make_async_copy(node_in, node, sems.at[0]),
        pltpu.make_async_copy(grad_in, paired.at[pl.ds(0, width), :], sems.at[1]),
        pltpu.make_async_copy(hess_in, paired.at[pl.ds(width, width), :], sems.at[2]),
    ]
    large = [
        pltpu.make_async_copy(
            bins_in.at[pl.ds(i * step, step), :], raw.at[pl.ds(i * step, step), :], sems.at[3 + i]
        )
        for i in range(blocks)
    ]
    for copy in small + large:
        copy.start()
    for copy in small:
        copy.wait()
    for slot in range(NODES):
        here = (node[...] == (core ^ slot)).astype(jnp.float32)
        spread[slot * 2 * K : (slot + 1) * 2 * K, :] = (
            paired[...].astype(jnp.float32) * here
        ).astype(jnp.bfloat16)
    for i, copy in enumerate(large):
        copy.wait()
        at = slice(i * step, (i + 1) * step)
        bins[at, :] = raw[at, :].astype(jnp.float32).astype(jnp.bfloat16)
    hist_body(plan, path, 0, count, True, bins, spread, keep, send)


def next_kernel(plan, path, first_unit, count, bins, spread, keep, send):
    hist_body(plan, path, first_unit, count, False, bins, spread, keep, send)


class Chain:
    def __init__(self):
        self.last = None

    def __call__(
        self, body, out_shape, operands, flops=10**10, in_place=None, out_place=None, **more
    ):
        n = len(operands)
        spec = {
            True: pl.BlockSpec(memory_space=pltpu.VMEM),
            False: pl.BlockSpec(memory_space=pl.ANY),
            None: pl.BlockSpec(memory_space=pltpu.HBM),
        }
        in_specs = [spec[x] for x in in_place or [True] * n]
        out_specs = [spec[x] for x in out_place or [True] * len(out_shape)]
        operands = list(operands)
        if self.last is not None:
            in_specs.append(spec[False])
            operands.append(self.last)

            def run(*refs):
                body(*refs[:n], *refs[n + 1 :])
        else:
            run = body
        outs = pl.pallas_call(
            run,
            out_shape=out_shape,
            in_specs=in_specs,
            out_specs=out_specs,
            compiler_params=pltpu.CompilerParams(vmem_limit_bytes=VMEM_LIMIT),
            cost_estimate=pl.CostEstimate(flops=flops, bytes_accessed=1024, transcendentals=0),
            **more,
        )(*operands)
        self.last = outs[-1]
        return outs


def f32(*shape):
    return jax.ShapeDtypeStruct(shape, jnp.float32)


def add_body(n_outs, *refs):
    parts, outs = refs[:-n_outs], refs[-n_outs:]
    each = outs[0].shape[0]
    row = 0
    for mine, theirs in zip(parts[::2], parts[1::2], strict=True):
        rows = mine.shape[1]
        for i, out in enumerate(outs):
            at = slice(i * each, (i + 1) * each)
            out[:, row : row + rows, :] = mine[at] + theirs[at]
        row += rows


def join_body(*refs):
    parts, out = refs[:-1], refs[-1]
    each = out.shape[0] // len(parts)
    for i, part in enumerate(parts):
        out[i * each : (i + 1) * each] = part[...]


def score(g, h):
    return g * g / (h + RIDGE)


def curves_body(sizes, n_parts, first_unit, has_totals, last, *refs):
    n = sum(n for n, _ in n_parts)
    parts, refs = refs[:n], refs[n:]
    if has_totals:
        weights, *refs = refs
        if not last:
            totals, gains = refs
    elif last:
        packed, old_gains, weights = refs
    else:
        packed, old_gains, weights, gains = refs
    width = weights.shape[2]
    row = lax.broadcasted_iota(jnp.int32, (EXTRA, width), 0)

    def summed(mine, start):
        total = mine[0][0, start : start + EXTRA, :]
        for part in mine[1:]:
            total += part[0, start : start + EXTRA, :]
        return total

    if has_totals:
        block = summed(parts[: n_parts[0][0]], sizes[0] * 2 * K)
        gain_rows = jnp.zeros((EXTRA, width), jnp.float32)
        if not last:
            totals[...] = block
    else:
        block = packed[...]
        gain_rows = old_gains[...]
    columns = [
        jnp.broadcast_to(block[:, i : i + 1], (EXTRA, width)) for i in range(2 * K // EXTRA)
    ]
    unit = 0
    taken = 0
    for n, chunks in n_parts:
        mine = parts[taken : taken + n]
        taken += n
        at = 0
        for chunk in chunks:
            for u in range(sizes[chunk]):
                gain = jnp.zeros((EXTRA, width), jnp.float32)
                for i in range(K // EXTRA):
                    gl = summed(mine, at + i * EXTRA)
                    hl = summed(mine, at + K + i * EXTRA)
                    g, h = columns[i], columns[K // EXTRA + i]
                    gain += score(gl, hl) + score(g - gl, h - hl) - score(g, h)
                    to = unit * K + i * EXTRA
                    weights[0, to : to + EXTRA, :] = -gl / (hl + RIDGE)
                mean = jnp.sum(gain, axis=0, keepdims=True) / K
                gain_rows = jnp.where(row == first_unit + unit, mean, gain_rows)
                at += 2 * K
                unit += 1
            if has_totals and chunk == 0:
                at += EXTRA
    if last:
        weights[0, unit * K : unit * K + EXTRA, :] = gain_rows
    else:
        gains[...] = gain_rows


def place_body(plan, path, first_unit, count, last, first, *refs):
    if not first:
        refs = refs[1:]
    mine, theirs, weights = refs[:3]
    if last:
        gains, held, lines, sems, held_sems = refs[3:]
    else:
        token, sems = refs[3:]
        token[...] = jnp.zeros_like(token)
    me = lax.axis_index("dp")
    copies = []
    fetched = []
    for side, source in enumerate((mine, theirs)):
        who = me ^ side
        if last:
            fetch = pltpu.make_async_copy(
                source.at[:, pl.ds(count * K, EXTRA), :], held.at[side], held_sems.at[side]
            )
            fetch.start()
            fetched.append(fetch)
        for item in range(plan.items):
            own = low_bin(path, who, item)
            copy = pltpu.make_async_copy(
                source.at[item, pl.ds(0, count * K), :].reshape(count, K, source.shape[2]),
                weights.at[who & 1, pl.ds(first_unit, count), own],
                sems.at[side * plan.items + item],
            )
            copy.start()
            copies.append(copy)
    if last:
        for side in range(2):
            fetched[side].wait()
        for side in range(2):
            who = me ^ side
            for item in range(plan.items):
                own = low_bin(path, who, item)
                for h in range(lines.shape[0]):
                    lines[h, who & 1, own] = held[side, item, :, h * LANES : (h + 1) * LANES]
        for h in range(lines.shape[0]):
            for node in range(NODES):
                for u in range(plan.units):
                    gains[node, u * plan.unit : (u + 1) * plan.unit, h * LANES : (h + 1) * LANES] = lines[
                        h, node, :, u, :
                    ]
    for copy in copies:
        copy.wait()


def on_device(bin_index, node_ids, gradients, hessians):
    devices = lax.axis_size("dp")
    plan = Plan(devices)
    rows, features = bin_index.shape
    width = gradients.shape[1]
    chain = Chain()

    def swap(x, partner):
        return lax.ppermute(x, "dp", [(d, partner(d)) for d in range(devices)])

    def swap_stage(x, stage):
        return swap(x, lambda d: d ^ stage[d & 1])

    def swap_cores(x):
        return swap(x, lambda d: d ^ 1)

    def swap_top(x):
        return swap(x, lambda d: d ^ plan.top)

    sizes, batches = plan.sizes, plan.batches
    starts = [sum(sizes[:i]) for i in range(len(sizes))]
    n_stages = plan.n_stages
    got = {}
    shared = {}

    def depth(chunk):
        return sizes[chunk] * 2 * K + (EXTRA if chunk == 0 else 0)

    def add(pair, n_outs):
        items, height, _ = pair[0].shape
        return chain(
            functools.partial(add_body, n_outs), [f32(items // n_outs, height, features)] * n_outs, pair
        )

    def histogram(c):
        halves = [f32(plan.items, depth(c), features)] * 2
        if c == 0:
            blocks = 8
            keep, send, bins, spread = chain(
                functools.partial(first_kernel, plan, plan.halve[c], sizes[c], blocks),
                [
                    *halves,
                    jax.ShapeDtypeStruct((rows, features), jnp.bfloat16),
                    jax.ShapeDtypeStruct((NODES * 2 * K, rows), jnp.bfloat16),
                ],
                [
                    pltpu.with_memory_space_constraint(x, pltpu.HBM)
                    for x in (bin_index, node_ids.reshape(1, rows), gradients.T, hessians.T)
                ],
                in_place=[None] * 4,
                scratch_shapes=[
                    pltpu.VMEM((rows, features), jnp.int32),
                    pltpu.VMEM((1, rows), jnp.int32),
                    pltpu.VMEM((2 * width, rows), jnp.bfloat16),
                    pltpu.SemaphoreType.DMA((3 + blocks,)),
                ],
            )
            shared["data"] = (bins, spread)
        else:
            keep, send = chain(
                functools.partial(next_kernel, plan, plan.halve[c], starts[c], sizes[c]),
                halves,
                shared["data"],
                flops=10**10,
            )
        got[c] = [keep, swap_cores(send)]

    def reduce(c, stage):
        if stage < n_stages:
            mine, other = add(got[c], 2)
            got[c] = [mine, swap_stage(other, plan.halve[c][stage])]
        else:
            (mine,) = add(got[c], 1)
            got[c] = [mine, swap_top(mine)]

    def curves(g):
        chunks = batches[g]
        count = sum(sizes[c] for c in chunks)
        last = g == len(batches) - 1
        parts = sum((got[c] for c in chunks), [])
        n_parts = [(2, [c]) for c in chunks]
        outs = [f32(1, count * K + (EXTRA if last else 0), features)]
        if not last:
            outs += [f32(EXTRA, features)] * (2 if g == 0 else 1)
        extra = [] if g == 0 else [shared["totals"], shared["gains"]]
        outs = chain(
            functools.partial(curves_body, sizes, n_parts, starts[chunks[0]], g == 0, last),
            outs,
            parts + extra,
        )
        if not last:
            shared["gains"] = outs[-1]
            if g == 0:
                shared["totals"] = outs[1]
        got["G", g] = [outs[0], swap_stage(outs[0], plan.gather[g][-1])]

    def gather(g, stage):
        parts = got["G", g]
        items, height, _ = parts[0].shape
        (joined,) = chain(join_body, [f32(2 * items, height, features)], parts)
        if stage:
            got["G", g] = [joined, swap_stage(joined, plan.gather[g][stage - 1])]
        else:
            got["G", g] = [joined, swap_cores(joined)]

    def place(g):
        chunks = batches[g]
        count = sum(sizes[c] for c in chunks)
        last = g == len(batches) - 1
        out_shape = [f32(NODES, plan.units, plan.unit, K, features), f32(EXTRA, LANES)]
        scratch = [pltpu.SemaphoreType.DMA((2 * plan.items,))]
        if last:
            out_shape[1] = f32(NODES, B, features)
            scratch = [
                pltpu.VMEM((2, plan.items, EXTRA, features), jnp.float32),
                pltpu.VMEM((features // LANES, NODES, plan.unit, EXTRA, LANES), jnp.float32),
                *scratch,
                pltpu.SemaphoreType.DMA((2,)),
            ]
        buffer = [] if g == 0 else [shared["weights"]]
        operands = [*buffer, *got["G", g]]
        shared["weights"], shared["gains_out"] = chain(
            functools.partial(place_body, plan, plan.gather[g], starts[chunks[0]], count, last, g == 0),
            out_shape,
            operands,
            in_place=[None] * len(buffer) + [False] * 2,
            out_place=[None, True],
            scratch_shapes=scratch,
            input_output_aliases={0: 0} if buffer else {},
        )

    tasks = []
    for c in range(len(sizes)):
        tasks.append((c - 0.2, ("K", c)))
        for stage in range(n_stages + 1):
            tasks.append((c + 1 + 1.02 * stage, ("S", c, stage)))
    for g, chunks in enumerate(batches):
        at = chunks[-1] + n_stages + 2.1 - (0.5 if g < len(batches) - 1 else 0)
        tasks.append((at, ("R", g)))
        for i, stage in enumerate(reversed(range(n_stages))):
            tasks.append((at + 1 + i, ("G", g, stage)))
        tasks.append((at + 1 + n_stages, ("P", g)))
    kinds = {"K": histogram, "S": reduce, "R": curves, "G": gather, "P": place}
    for name, *arguments in plan.order or [task for _, task in sorted(tasks, key=lambda t: t[0])]:
        kinds[name](*arguments)
    weights = shared["weights"].reshape(NODES, B, K, features)
    return shared["gains_out"].transpose(2, 0, 1), weights.transpose(3, 0, 1, 2)


def solution(mesh):
    return jax.shard_map(
        on_device,
        mesh=mesh,
        in_specs=(P("dp", None), P("dp"), P("dp", None), P("dp", None)),
        out_specs=(P(), P()),
        check_vma=False,
    )
```

```python
import functools

import jax
import jax.numpy as jnp
from jax import lax
from jax.experimental import pallas as pl
from jax.experimental.pallas import tpu as pltpu
from jax.sharding import PartitionSpec as P

B = 64
K = 32
NODES = 2
RIDGE = 1.0
LANES = 128
EXTRA = 8
VMEM_LIMIT = 48 * 2**20
SIZES = [1, 1, 2, 2, 2]
BATCHES = [[0, 1], [2], [3], [4]]
HALVE = [('zxy', 'zyx'), ('zxy', 'zyx'), ('xzy', 'yzx'), ('xzy', 'yzx'), ('xyz', 'yxz')]
GATHER = [('xzy', 'yzx'), ('xzy', 'yzx'), ('zxy', 'zyx'), ('xyz', 'yxz')]
ORDER = [('K', 0), ('K', 2), ('S', 0, 0), ('K', 1), ('S', 2, 0), ('K', 3), ('S', 1, 0), ('S', 0, 1), ('S', 3, 0), ('K', 4), ('S', 2, 1), ('S', 1, 1), ('S', 0, 2), ('S', 4, 0), ('S', 3, 1), ('S', 0, 3), ('S', 1, 2), ('S', 2, 2), ('S', 4, 1), ('S', 1, 3), ('S', 2, 3), ('S', 3, 2), ('S', 4, 2), ('R', 0), ('S', 3, 3), ('G', 0, 2), ('R', 1), ('S', 4, 3), ('R', 2), ('G', 1, 2), ('G', 2, 2), ('R', 3), ('G', 0, 1), ('G', 2, 1), ('G', 3, 2), ('G', 1, 1), ('G', 0, 0), ('G', 3, 1), ('G', 1, 0), ('G', 2, 0), ('P', 0), ('P', 1), ('G', 3, 0), ('P', 2), ('P', 3)]
DOTS = 8
FLIP = {"x": 2, "y": 4, "z": 8}


class Plan:
    def __init__(self, devices):
        bits = devices.bit_length() - 1
        assert devices == 1 << bits and bits >= 4
        self.top = devices // 2
        self.unit = self.items = devices // 4
        self.units = B // self.unit
        assert 1 <= self.units <= EXTRA
        self.n_stages = bits - 2
        if devices == 32 and self.units == sum(SIZES):
            self.sizes, self.batches, self.order = SIZES, BATCHES, ORDER
            self.halve = [self.paths(*pair) for pair in HALVE]
            self.gather = [self.paths(*pair) for pair in GATHER]
        else:
            self.sizes, self.batches, self.order = [self.units], [[0]], []
            later = [(1 << b, 1 << b) for b in range(3, bits - 1)]
            self.halve = self.gather = [[(2, 4), (4, 2), *later]]

    def paths(self, even, odd):
        return [(FLIP[e], FLIP[o]) for e, o in zip(even, odd, strict=True)]


def mask(path, item, core):
    total = 0
    for i, (even, odd) in enumerate(reversed(path)):
        total = total ^ (((item >> i) & 1) * (even + core * (odd - even)))
    return total


def low_bin(path, device, item):
    return ((device ^ mask(path, item, device & 1)) >> 1) & ((1 << len(path)) - 1)


def mirrored(path, item, core):
    even, odd = ([stage[c] for stage in reversed(path)] for c in (0, 1))
    total = 0
    for i in range(len(path)):
        on_even, on_odd = 1 << odd.index(even[i]), 1 << even.index(odd[i])
        total = total ^ (((item >> i) & 1) * (on_even + core * (on_odd - on_even)))
    return total


def hist_body(plan, path, first_unit, count, has_totals, bins, spread, keep, send):
    me = lax.axis_index("dp")
    rows = bins.shape[0]
    step = min(rows, 256)

    def one(item):
        own = low_bin(path, me, item)
        theirs = mirrored(path, item, me & 1)
        for u in range(count):
            level = (first_unit + u) * plan.unit + own
            level = level.astype(jnp.float32).astype(jnp.bfloat16)
            total = jnp.zeros((spread.shape[0], bins.shape[1]), jnp.float32)
            for start in range(0, rows, step):
                below = jnp.where(
                    bins[start : start + step, :] <= level, jnp.bfloat16(1), jnp.bfloat16(0)
                )
                total += jnp.dot(
                    spread[:, start : start + step], below, preferred_element_type=jnp.float32
                )
            at = pl.ds(u * 2 * K, 2 * K)
            keep[item, at, :] = total[: 2 * K, :]
            send[theirs, at, :] = total[2 * K :, :]

    together = min(plan.items, max(1, DOTS // count))

    @pl.loop(0, plan.items // together)
    def _(turn):
        for i in range(together):
            one(turn * together + i)

    if has_totals:
        sums = jnp.sum(spread[...].astype(jnp.float32), axis=1, keepdims=True)
        lane = lax.broadcasted_iota(jnp.int32, (EXTRA, bins.shape[1]), 1)
        for target, base in ((keep, 0), (send, 2 * K)):
            packed = jnp.zeros((EXTRA, bins.shape[1]), jnp.float32)
            for i in range(2 * K // EXTRA):
                part = sums[base + i * EXTRA : base + (i + 1) * EXTRA, :]
                packed = jnp.where(lane == i, part, packed)
            for item in range(plan.items):
                target[item, pl.ds(count * 2 * K, EXTRA), :] = packed


def first_kernel(plan, path, count, blocks, *refs):
    bins_in, node_in, grad_in, hess_in, keep, send, bins, spread = refs[:8]
    raw, node, paired, sems = refs[8:]
    me = lax.axis_index("dp")
    core = me & 1
    step = bins.shape[0] // blocks
    width = grad_in.shape[0]
    small = [
        pltpu.make_async_copy(node_in, node, sems.at[0]),
        pltpu.make_async_copy(grad_in, paired.at[pl.ds(0, width), :], sems.at[1]),
        pltpu.make_async_copy(hess_in, paired.at[pl.ds(width, width), :], sems.at[2]),
    ]
    large = [
        pltpu.make_async_copy(
            bins_in.at[pl.ds(i * step, step), :], raw.at[pl.ds(i * step, step), :], sems.at[3 + i]
        )
        for i in range(blocks)
    ]
    for copy in small + large:
        copy.start()
    for copy in small:
        copy.wait()
    for slot in range(NODES):
        here = (node[...] == (core ^ slot)).astype(jnp.float32)
        spread[slot * 2 * K : (slot + 1) * 2 * K, :] = (
            paired[...].astype(jnp.float32) * here
        ).astype(jnp.bfloat16)
    for i, copy in enumerate(large):
        copy.wait()
        at = slice(i * step, (i + 1) * step)
        bins[at, :] = raw[at, :].astype(jnp.float32).astype(jnp.bfloat16)
    hist_body(plan, path, 0, count, True, bins, spread, keep, send)


def next_kernel(plan, path, first_unit, count, bins, spread, keep, send):
    hist_body(plan, path, first_unit, count, False, bins, spread, keep, send)


class Chain:
    def __init__(self):
        self.last = None

    def __call__(
        self, body, out_shape, operands, flops=10**10, in_place=None, out_place=None, **more
    ):
        n = len(operands)
        spec = {
            True: pl.BlockSpec(memory_space=pltpu.VMEM),
            False: pl.BlockSpec(memory_space=pl.ANY),
            None: pl.BlockSpec(memory_space=pltpu.HBM),
        }
        in_specs = [spec[x] for x in in_place or [True] * n]
        out_specs = [spec[x] for x in out_place or [True] * len(out_shape)]
        operands = list(operands)
        if self.last is not None:
            in_specs.append(spec[False])
            operands.append(self.last)

            def run(*refs):
                body(*refs[:n], *refs[n + 1 :])
        else:
            run = body
        outs = pl.pallas_call(
            run,
            out_shape=out_shape,
            in_specs=in_specs,
            out_specs=out_specs,
            compiler_params=pltpu.CompilerParams(vmem_limit_bytes=VMEM_LIMIT),
            cost_estimate=pl.CostEstimate(flops=flops, bytes_accessed=1024, transcendentals=0),
            **more,
        )(*operands)
        self.last = outs[-1]
        return outs


def f32(*shape):
    return jax.ShapeDtypeStruct(shape, jnp.float32)


def add_body(n_outs, *refs):
    parts, outs = refs[:-n_outs], refs[-n_outs:]
    each = outs[0].shape[0]
    row = 0
    for mine, theirs in zip(parts[::2], parts[1::2], strict=True):
        rows = mine.shape[1]
        for i, out in enumerate(outs):
            at = slice(i * each, (i + 1) * each)
            out[:, row : row + rows, :] = mine[at] + theirs[at]
        row += rows


def join_body(*refs):
    parts, out = refs[:-1], refs[-1]
    each = out.shape[0] // len(parts)
    for i, part in enumerate(parts):
        out[i * each : (i + 1) * each] = part[...]


def score(g, h):
    return g * g / (h + RIDGE)


def curves_body(sizes, n_parts, first_unit, has_totals, last, *refs):
    n = sum(n for n, _ in n_parts)
    parts, refs = refs[:n], refs[n:]
    if has_totals:
        weights, *refs = refs
        if not last:
            totals, gains = refs
    elif last:
        packed, old_gains, weights = refs
    else:
        packed, old_gains, weights, gains = refs
    width = weights.shape[2]
    row = lax.broadcasted_iota(jnp.int32, (EXTRA, width), 0)

    def summed(mine, start):
        total = mine[0][0, start : start + EXTRA, :]
        for part in mine[1:]:
            total += part[0, start : start + EXTRA, :]
        return total

    if has_totals:
        block = summed(parts[: n_parts[0][0]], sizes[0] * 2 * K)
        gain_rows = jnp.zeros((EXTRA, width), jnp.float32)
        if not last:
            totals[...] = block
    else:
        block = packed[...]
        gain_rows = old_gains[...]
    columns = [
        jnp.broadcast_to(block[:, i : i + 1], (EXTRA, width)) for i in range(2 * K // EXTRA)
    ]
    unit = 0
    taken = 0
    for n, chunks in n_parts:
        mine = parts[taken : taken + n]
        taken += n
        at = 0
        for chunk in chunks:
            for u in range(sizes[chunk]):
                gain = jnp.zeros((EXTRA, width), jnp.float32)
                for i in range(K // EXTRA):
                    gl = summed(mine, at + i * EXTRA)
                    hl = summed(mine, at + K + i * EXTRA)
                    g, h = columns[i], columns[K // EXTRA + i]
                    gain += score(gl, hl) + score(g - gl, h - hl) - score(g, h)
                    to = unit * K + i * EXTRA
                    weights[0, to : to + EXTRA, :] = -gl / (hl + RIDGE)
                mean = jnp.sum(gain, axis=0, keepdims=True) / K
                gain_rows = jnp.where(row == first_unit + unit, mean, gain_rows)
                at += 2 * K
                unit += 1
            if has_totals and chunk == 0:
                at += EXTRA
    if last:
        weights[0, unit * K : unit * K + EXTRA, :] = gain_rows
    else:
        gains[...] = gain_rows


def place_body(plan, path, first_unit, count, last, first, *refs):
    if not first:
        refs = refs[1:]
    mine, theirs, weights = refs[:3]
    if last:
        gains, held, lines, sems, held_sems = refs[3:]
    else:
        token, sems = refs[3:]
        token[...] = jnp.zeros_like(token)
    me = lax.axis_index("dp")
    copies = []
    fetched = []
    for side, source in enumerate((mine, theirs)):
        who = me ^ side
        if last:
            fetch = pltpu.make_async_copy(
                source.at[:, pl.ds(count * K, EXTRA), :], held.at[side], held_sems.at[side]
            )
            fetch.start()
            fetched.append(fetch)
        for item in range(plan.items):
            own = low_bin(path, who, item)
            copy = pltpu.make_async_copy(
                source.at[item, pl.ds(0, count * K), :].reshape(count, K, source.shape[2]),
                weights.at[who & 1, pl.ds(first_unit, count), own],
                sems.at[side * plan.items + item],
            )
            copy.start()
            copies.append(copy)
    if last:
        for side in range(2):
            fetched[side].wait()
        for side in range(2):
            who = me ^ side
            for item in range(plan.items):
                own = low_bin(path, who, item)
                for h in range(lines.shape[0]):
                    lines[h, who & 1, own] = held[side, item, :, h * LANES : (h + 1) * LANES]
        for h in range(lines.shape[0]):
            for node in range(NODES):
                for u in range(plan.units):
                    gains[node, u * plan.unit : (u + 1) * plan.unit, h * LANES : (h + 1) * LANES] = lines[
                        h, node, :, u, :
                    ]
    for copy in copies:
        copy.wait()


def on_device(bin_index, node_ids, gradients, hessians):
    devices = lax.axis_size("dp")
    plan = Plan(devices)
    rows, features = bin_index.shape
    width = gradients.shape[1]
    chain = Chain()

    def swap(x, partner):
        return lax.ppermute(x, "dp", [(d, partner(d)) for d in range(devices)])

    def swap_stage(x, stage):
        return swap(x, lambda d: d ^ stage[d & 1])

    def swap_cores(x):
        return swap(x, lambda d: d ^ 1)

    def swap_top(x):
        return swap(x, lambda d: d ^ plan.top)

    sizes, batches = plan.sizes, plan.batches
    starts = [sum(sizes[:i]) for i in range(len(sizes))]
    n_stages = plan.n_stages
    got = {}
    shared = {}

    def depth(chunk):
        return sizes[chunk] * 2 * K + (EXTRA if chunk == 0 else 0)

    def add(pair, n_outs):
        items, height, _ = pair[0].shape
        return chain(
            functools.partial(add_body, n_outs), [f32(items // n_outs, height, features)] * n_outs, pair
        )

    def histogram(c):
        halves = [f32(plan.items, depth(c), features)] * 2
        if c == 0:
            blocks = 2
            keep, send, bins, spread = chain(
                functools.partial(first_kernel, plan, plan.halve[c], sizes[c], blocks),
                [
                    *halves,
                    jax.ShapeDtypeStruct((rows, features), jnp.bfloat16),
                    jax.ShapeDtypeStruct((NODES * 2 * K, rows), jnp.bfloat16),
                ],
                [
                    pltpu.with_memory_space_constraint(x, pltpu.HBM)
                    for x in (bin_index, node_ids.reshape(1, rows), gradients.T, hessians.T)
                ],
                in_place=[None] * 4,
                scratch_shapes=[
                    pltpu.VMEM((rows, features), jnp.int32),
                    pltpu.VMEM((1, rows), jnp.int32),
                    pltpu.VMEM((2 * width, rows), jnp.bfloat16),
                    pltpu.SemaphoreType.DMA((3 + blocks,)),
                ],
            )
            shared["data"] = (bins, spread)
        else:
            keep, send = chain(
                functools.partial(next_kernel, plan, plan.halve[c], starts[c], sizes[c]),
                halves,
                shared["data"],
                flops=10**10,
            )
        got[c] = [keep, swap_cores(send)]

    def reduce(c, stage):
        if stage < n_stages:
            mine, other = add(got[c], 2)
            got[c] = [mine, swap_stage(other, plan.halve[c][stage])]
        else:
            (mine,) = add(got[c], 1)
            got[c] = [mine, swap_top(mine)]

    def curves(g):
        chunks = batches[g]
        count = sum(sizes[c] for c in chunks)
        last = g == len(batches) - 1
        parts = sum((got[c] for c in chunks), [])
        n_parts = [(2, [c]) for c in chunks]
        outs = [f32(1, count * K + (EXTRA if last else 0), features)]
        if not last:
            outs += [f32(EXTRA, features)] * (2 if g == 0 else 1)
        extra = [] if g == 0 else [shared["totals"], shared["gains"]]
        outs = chain(
            functools.partial(curves_body, sizes, n_parts, starts[chunks[0]], g == 0, last),
            outs,
            parts + extra,
        )
        if not last:
            shared["gains"] = outs[-1]
            if g == 0:
                shared["totals"] = outs[1]
        got["G", g] = [outs[0], swap_stage(outs[0], plan.gather[g][-1])]

    def gather(g, stage):
        parts = got["G", g]
        items, height, _ = parts[0].shape
        (joined,) = chain(join_body, [f32(2 * items, height, features)], parts)
        if stage:
            got["G", g] = [joined, swap_stage(joined, plan.gather[g][stage - 1])]
        else:
            got["G", g] = [joined, swap_cores(joined)]

    def place(g):
        chunks = batches[g]
        count = sum(sizes[c] for c in chunks)
        last = g == len(batches) - 1
        out_shape = [f32(NODES, plan.units, plan.unit, K, features), f32(EXTRA, LANES)]
        scratch = [pltpu.SemaphoreType.DMA((2 * plan.items,))]
        if last:
            out_shape[1] = f32(NODES, B, features)
            scratch = [
                pltpu.VMEM((2, plan.items, EXTRA, features), jnp.float32),
                pltpu.VMEM((features // LANES, NODES, plan.unit, EXTRA, LANES), jnp.float32),
                *scratch,
                pltpu.SemaphoreType.DMA((2,)),
            ]
        buffer = [] if g == 0 else [shared["weights"]]
        operands = [*buffer, *got["G", g]]
        shared["weights"], shared["gains_out"] = chain(
            functools.partial(place_body, plan, plan.gather[g], starts[chunks[0]], count, last, g == 0),
            out_shape,
            operands,
            in_place=[None] * len(buffer) + [False] * 2,
            out_place=[None, True],
            scratch_shapes=scratch,
            input_output_aliases={0: 0} if buffer else {},
        )

    tasks = []
    for c in range(len(sizes)):
        tasks.append((c - 0.2, ("K", c)))
        for stage in range(n_stages + 1):
            tasks.append((c + 1 + 1.02 * stage, ("S", c, stage)))
    for g, chunks in enumerate(batches):
        at = chunks[-1] + n_stages + 2.1 - (0.5 if g < len(batches) - 1 else 0)
        tasks.append((at, ("R", g)))
        for i, stage in enumerate(reversed(range(n_stages))):
            tasks.append((at + 1 + i, ("G", g, stage)))
        tasks.append((at + 1 + n_stages, ("P", g)))
    kinds = {"K": histogram, "S": reduce, "R": curves, "G": gather, "P": place}
    for name, *arguments in plan.order or [task for _, task in sorted(tasks, key=lambda t: t[0])]:
        kinds[name](*arguments)
    weights = shared["weights"].reshape(NODES, B, K, features)
    return shared["gains_out"].transpose(2, 0, 1), weights.transpose(3, 0, 1, 2)


def solution(mesh):
    return jax.shard_map(
        on_device,
        mesh=mesh,
        in_specs=(P("dp", None), P("dp"), P("dp", None), P("dp", None)),
        out_specs=(P(), P()),
        check_vma=False,
    )
```
